32 devices in a mesh: groups: 2 (over y), tm: 4 (over z), space: 2 (over x), chan: 2 (over core).
Axes of the slice: x: 2, y: 2, z: 4, core: 2. Of those that a mesh axis runs over, the one named last changes fastest.
Arguments:
- frames: bfloat16 [32, 64, 64, 256], P(('groups', 'tm'), 'chan', 'space'), parts along dimension 0, may hold values from -6 to 6
- conv_taps: float32 [64, 9], P('chan'), may hold values from -2 to 2
- pooling: float32 [64, 256], P('space'), may hold values from -0.0625 to 0.0625
- gain_matrix: float32 [256, 128], P(None, ('space', 'chan')), may hold values from -0.5 to 0.5
- transition: float32 [256, 256], replicated, as said below
- update_map: float32 [256, 256], replicated, as said below
- quiet_root: float32 [256, 256], replicated, as said below
- observed_root: float32 [256, 256], replicated, as said below
- init_mean: float32 [512], P('groups'), parts along dimension 0, may hold values from -6 to 6
- init_root: float32 [512, 256], P('groups'), parts along dimension 0, as said below
- observed: int32 [32], P(('groups', 'tm')), parts along dimension 0, may hold values 0 or 1
Outputs:
- filtered_means: float32 [32, 256], P(('groups', 'tm')), parts along dimension 0
- block_roots: float32 [8, 256, 256], P(('groups', 'tm')), parts along dimension 0
- tap_gradient: float32 [8, 64, 9], P(('groups', 'tm'), 'chan'), parts along dimension 0
The draws below stay inside these ranges and needn't reach their ends.
There are 2 independent parts, one for each index of `groups`. The reference program is written for one: setup_inputs(seed, part) draws one part's arguments, and reference() takes and returns one part's arrays. A program takes and returns all parts, laid end to end along the dimension named above; an argument that names none is the same for every part. Nothing has to cross between parts.
Inputs may be any that keep to these rules, and one draw needn't show every extreme that they name: transition and update_map are upper triangular, with the same diagonal entries where these exceed 0.8. transition is upper triangular. `quiet_root`: upper triangular with a positive diagonal. `observed_root`: upper triangular with a positive diagonal. `init_root`: upper triangular with a positive diagonal.
All inputs are finite; a program needn't handle non-finite values. No bound on the sum of `observed` on one device may be relied on, other than what follows from the above.
Results may differ from the reference program's by a relative error of at most 0.0003.
Values may be sent and summed in bfloat16 or wider, within the bound.
A program may use at most 64 MiB of HBM per device.

```python
import math
import jax
import jax.numpy as jnp
from jax import lax

S = 256
CH = 64
W = 256
DILATION_STEP = 2
TB = 4
ROWS_DEV = 32
NT = 16
H = 64
OBS = 128
N_TM = 4
N_SPACE = 2


def channel_rates(key):
    pick_key = jax.random.fold_in(key, 101)
    level_key = jax.random.fold_in(key, 102)
    fast_key = jax.random.fold_in(key, 103)
    slow_share = 0.5
    is_slow = jax.random.uniform(pick_key, (S,), jnp.float32) < slow_share
    slow_rates = 0.1 ** (jax.random.uniform(level_key, (S,), jnp.float32, 0.2, 0.5) / NT)
    fast_rates = jax.random.uniform(fast_key, (S,), jnp.float32, 0.3, 0.7)
    return jnp.where(is_slow, slow_rates, fast_rates)


def coupled(key, rates, spread):
    entries = jax.random.normal(key, (S, S), jnp.float32) * (spread / math.sqrt(S))
    damping = 1.0 - rates[:, None] * rates[None, :]
    return jnp.diag(rates) + jnp.triu(entries * damping, 1)


def triangular_root(key):
    diag_key = jax.random.fold_in(key, 301)
    off_key = jax.random.fold_in(key, 302)
    upper_end = 0.6
    levels = jax.random.uniform(diag_key, (S,), jnp.float32, math.log(0.3), math.log(upper_end))
    entries = jax.random.normal(off_key, (S, S), jnp.float32) * (0.15 / math.sqrt(S))
    return jnp.diag(jnp.exp(levels)) + jnp.triu(entries, 1)


def draw_transition(key, part):
    rates = channel_rates(key)
    return coupled(jax.random.fold_in(key, 201), rates, 0.4)


def draw_update_map(key, part):
    rates = channel_rates(key)
    shrink = jax.random.uniform(jax.random.fold_in(key, 202), (S,), jnp.float32, 0.5, 1.0)
    shrunk = jnp.where(rates > 0.8, rates, rates * shrink)
    return coupled(jax.random.fold_in(key, 203), shrunk, 0.4)


def draw_quiet_root(key, part):
    return triangular_root(jax.random.fold_in(key, 1))


def draw_observed_root(key, part):
    return triangular_root(jax.random.fold_in(key, 2))


def draw_init_root(key, part):
    return triangular_root(jax.random.fold_in(key, 3))


def touch_ends(values, key, smallest, top_value):
    place = [jax.random.randint(jax.random.fold_in(key, axis), (), 0, length) for axis, length in enumerate(values.shape)]
    main_axis = values.shape.index(max(values.shape))
    next_to = place[:main_axis] + [(place[main_axis] + 1) % values.shape[main_axis]] + place[main_axis + 1:]
    return values.at[tuple(place)].set(smallest).at[tuple(next_to)].set(top_value)


def block_levels(stream_key, dims, pieces, low, largest):
    def one(dim, shards_of):
        steps = jax.random.uniform(jax.random.fold_in(jax.random.fold_in(stream_key, 6), dim), (shards_of,), jnp.float32, low / len(pieces), largest / len(pieces))
        return jnp.repeat(jnp.exp(steps), dims[dim] // shards_of).reshape((-1,) + (1,) * (len(dims) - dim - 1))

    level = one(*pieces[0])
    for cut in pieces[1:]:
        level = level * one(*cut)
    return level


def centred(rng, extent, deviation, limit, cuts=(), kind=jnp.bfloat16):
    result = deviation * jax.random.normal(rng, extent, jnp.float32)
    if cuts:
        result = result * block_levels(rng, extent, cuts, -0.22, 0.18)
    return jnp.clip(result, -limit, limit).astype(kind)


def setup_inputs(seed: int = 0, part: int = 0) -> dict:
    splits = jax.random.split(jax.random.key(seed), 12)
    own_keys = jax.random.split(jax.random.fold_in(splits[11], part), 12)
    frames = centred(own_keys[0], (NT, CH, H, W), 1.0, 6.0, ((0, 4), (1, 2), (2, 2)))
    conv_taps = centred(splits[1], (CH, 9), 0.33, 2.0, ((0, 2),), jnp.float32)
    pooling = centred(splits[2], (H, W), (ROWS_DEV * W) ** -0.5, 0.0625, ((0, 2),), jnp.float32)
    gain_matrix = centred(splits[3], (S, OBS), OBS ** -0.5, 0.5, ((1, 4),), jnp.float32)
    transition = draw_transition(jax.random.fold_in(splits[11], 71), part)
    update_map = draw_update_map(jax.random.fold_in(splits[11], 71), part)
    quiet_root = draw_quiet_root(jax.random.fold_in(splits[11], 71), part)
    observed_root = draw_observed_root(jax.random.fold_in(splits[11], 71), part)
    init_mean = centred(own_keys[8], (S,), 1.0, 6.0, (), jnp.float32)
    init_root = draw_init_root(jax.random.fold_in(jax.random.fold_in(splits[11], part), 71), part)
    observed = touch_ends((jax.random.randint(own_keys[10], (NT,), 0, 2) < 1).astype(jnp.int32), jax.random.fold_in(own_keys[10], 1), 0, 1)
    return {"frames": frames, "conv_taps": conv_taps, "pooling": pooling, "gain_matrix": gain_matrix, "transition": transition, "update_map": update_map, "quiet_root": quiet_root, "observed_root": observed_root, "init_mean": init_mean, "init_root": init_root, "observed": observed}


precise = lax.Precision.HIGHEST

def upper_factor(gram_sum):
    is_blank = jnp.trace(gram_sum) == 0.0
    unit_matrix = jnp.eye(gram_sum.shape[0], dtype=jnp.float32)
    safe_gram = jnp.where(is_blank, unit_matrix, gram_sum)
    return jnp.where(is_blank, jnp.float32(0.0), jnp.linalg.cholesky(safe_gram).T)

def response_of(frame_advance, conv_taps):
    frame_height = frame_advance.shape[1]
    column_list = frame_advance.shape[2]
    padded_frame = jnp.pad(frame_advance.astype(jnp.float32), ((0, 0), (DILATION_STEP, DILATION_STEP), (DILATION_STEP, DILATION_STEP)))
    window_views = [padded_frame[:, left_element * DILATION_STEP:left_element * DILATION_STEP + frame_height, right_element * DILATION_STEP:right_element * DILATION_STEP + column_list] for left_element in range(3) for right_element in range(3)]
    response = jnp.zeros(frame_advance.shape, jnp.float32)
    for k in range(9):
        response = response + conv_taps[:, k][:, None, None] * window_views[k]
    return (response, window_views)

def reference(frames, conv_taps, pooling, gain_matrix, transition, update_map, quiet_root, observed_root, init_mean, init_root, observed):
    frame_height = frames.shape[2]
    column_list = frames.shape[3]
    pool_tiles = pooling.reshape(N_SPACE, ROWS_DEV, column_list)

    def per_step(inputs):
        frame_advance, flag = inputs
        response, window_views = response_of(frame_advance, conv_taps)
        tiles = response.reshape(CH, N_SPACE, ROWS_DEV, column_list)
        tile_sums = jnp.einsum('cshw,shw->sc', tiles, pool_tiles, precision=precise).reshape(N_SPACE * CH)
        weight = flag.astype(jnp.float32) / (frame_height * column_list)
        grad_step = jnp.stack([jnp.sum(response * window_views[k], axis=(1, 2)) for k in range(9)], axis=1) * weight
        return (tile_sums, grad_step)
    tile_sums, grad_steps = lax.map(per_step, (frames, observed))
    weights = observed.astype(jnp.float32)
    shifts = jnp.dot(tile_sums.astype(jnp.float32), gain_matrix.T.astype(jnp.float32), precision=precise, preferred_element_type=jnp.float32) * weights[:, None]
    tap_gradient = jnp.sum(grad_steps.reshape(N_TM, TB, CH, 9), axis=1)

    def advance(state, inputs):
        mean_now, root_now = state
        flag, shift_now = inputs
        step_map = jnp.where(flag > 0, update_map, transition)
        step_root = jnp.where(flag > 0, observed_root, quiet_root)
        mean_next = jnp.dot(step_map.astype(jnp.float32), mean_now.astype(jnp.float32), precision=precise, preferred_element_type=jnp.float32) + shift_now
        carried = jnp.dot(root_now.astype(jnp.float32), step_map.T.astype(jnp.float32), precision=precise, preferred_element_type=jnp.float32)
        gram_sum = jnp.dot(carried.T.astype(jnp.float32), carried.astype(jnp.float32), precision=precise, preferred_element_type=jnp.float32)
        gram_sum = gram_sum + jnp.dot(step_root.T.astype(jnp.float32), step_root.astype(jnp.float32), precision=precise, preferred_element_type=jnp.float32)
        root_next = upper_factor(gram_sum)
        return ((mean_next, root_next), (mean_next, root_next))
    final_state, outputs = lax.scan(advance, (init_mean, init_root), (observed, shifts))
    filtered_means, all_roots = outputs
    block_roots = all_roots[TB - 1::TB]
    return (filtered_means, block_roots, tap_gradient)
```

```python
import functools

import jax
import jax.numpy as jnp
from jax import lax
from jax.experimental import pallas as pl
from jax.experimental.pallas import tpu as pltpu
from jax.sharding import PartitionSpec as P

DILATION_STEP = 2
NB = 16
F32 = jnp.float32
BF16 = jnp.bfloat16
VMEM = pl.BlockSpec(memory_space=pltpu.VMEM)
SMEM = pl.BlockSpec(memory_space=pltpu.SMEM)

NT_DIMS = (((1,), (1,)), ((), ()))
TN_DIMS = (((0,), (0,)), ((), ()))
PAIRS = (((0, 0), 0), ((1, 1), 1), ((-1, -1), 2), ((0, 1), 3), ((-1, 0), 3), ((-1, 1), 4))


def moments_kernel(rows, group, position, inside, limit, flags, taps, x_ref, pools, taps_wide, grad_ref, sums_ref):
    steps, width = x_ref.shape[0], x_ref.shape[3]
    first = pl.program_id(0) * group
    for c in range(group):
        weight = taps[first + c, 0] * pools[0]
        for k in range(1, 9):
            weight = weight + taps[first + c, k] * pools[k]
        for t in range(steps):
            part = x_ref[t, c].astype(F32) * weight
            sums_ref[0, t * group + c : t * group + c + 1, :] = jnp.sum(part, axis=0, keepdims=True)
    lane = lax.broadcasted_iota(jnp.int32, (group * rows, width), 1)
    left, left_low, left_high, plain, by_one, by_two = [], [], [], [], [], []
    for t in range(steps):
        x = x_ref[t].reshape(group * rows, width).astype(F32)
        scaled = x * flags[t].astype(F32)
        left.append(scaled.astype(BF16))
        left_low.append(jnp.where(lane >= DILATION_STEP, scaled, 0.0).astype(BF16))
        left_high.append(jnp.where(lane < width - DILATION_STEP, scaled, 0.0).astype(BF16))
        plain.append(x.astype(BF16))
        one = pltpu.roll(x, width - DILATION_STEP, 1)
        by_one.append(jnp.where(lane < width - DILATION_STEP, one, 0.0).astype(BF16))
        two = pltpu.roll(x, width - 2 * DILATION_STEP, 1)
        by_two.append(jnp.where(lane < width - 2 * DILATION_STEP, two, 0.0).astype(BF16))
    cat = lambda pieces: jnp.concatenate(pieces, axis=1)
    left, plain = cat(left), cat(plain)
    size = group * rows
    lane_f = lax.broadcasted_iota(jnp.int32, (rows, size), 1)
    row_e = lax.broadcasted_iota(jnp.int32, (rows, size), 0)
    col_e = lax.rem(lane_f, rows)
    owner = lax.div(lane_f, rows)
    row_h, col_h = position(row_e), position(col_e)
    grads = [jnp.zeros((1, size), F32) for _ in range(9)]
    pairs = ((left, plain), (cat(left_low), plain), (cat(left_high), plain), (left, cat(by_one)), (left, cat(by_two)))
    for kind, (lhs, rhs) in enumerate(pairs):
        gram = lax.dot_general(lhs, rhs, NT_DIMS, preferred_element_type=F32)
        folded = jnp.zeros((rows, size), F32)
        for c in range(group):
            folded = jnp.where(owner == c, gram[c * rows : (c + 1) * rows, :], folded)
        for a in range(-1, 2):
            for z in range(-1, 2):
                h = row_h - DILATION_STEP * a
                keep = (h >= 0) & (h < limit) & (row_h - col_h == DILATION_STEP * (a - z)) & inside(row_e, col_e)
                row = jnp.sum(jnp.where(keep, folded, 0.0), axis=0, keepdims=True)
                for (b, y), which in PAIRS:
                    if which != kind:
                        continue
                    k, q = 3 * (a + 1) + b + 1, 3 * (z + 1) + y + 1
                    grads[k] = grads[k] + row * taps_wide[q : q + 1, :]
                    if b != y:
                        grads[q] = grads[q] + row * taps_wide[k : k + 1, :]
    for k in range(9):
        grad_ref[0, k : k + 1, :] = grads[k]


def moments(x, pools, conv_taps, flags, position, inside, limit):
    steps, channels, rows, width = x.shape
    group = min(channels, 256 // rows)
    groups = channels // group
    size = group * rows
    taps_wide = jnp.repeat(conv_taps.T, rows, axis=1)
    grads, sums = pl.pallas_call(
        functools.partial(moments_kernel, rows, group, position, inside, limit),
        grid=(groups,),
        in_specs=[
            SMEM,
            SMEM,
            pl.BlockSpec((steps, group, rows, width), lambda g: (0, g, 0, 0)),
            pl.BlockSpec((9, rows, width), lambda g: (0, 0, 0)),
            pl.BlockSpec((9, size), lambda g: (0, g)),
        ],
        out_specs=[
            pl.BlockSpec((1, 9, size), lambda g: (g, 0, 0)),
            pl.BlockSpec((1, steps * group, width), lambda g: (g, 0, 0)),
        ],
        out_shape=[
            jax.ShapeDtypeStruct((groups, 9, size), F32),
            jax.ShapeDtypeStruct((groups, steps * group, width), F32),
        ],
        compiler_params=pltpu.CompilerParams(vmem_limit_bytes=48 * 2**20),
        cost_estimate=pl.CostEstimate(flops=2 * 5 * groups * size * size * steps * width, bytes_accessed=x.size * 2, transcendentals=0),
    )(flags, conv_taps, x, pools, taps_wide)
    grads = jnp.sum(grads.reshape(groups, 9, group, rows), axis=3)
    sums = jnp.sum(sums, axis=2).reshape(groups, steps, group)
    return jnp.transpose(grads, (0, 2, 1)).reshape(channels, 9), jnp.transpose(sums, (1, 0, 2)).reshape(steps, channels)


def split2(x):
    high = x.astype(BF16)
    return high, (x - high.astype(F32)).astype(BF16)


def split3(x):
    high = x.astype(BF16)
    rest = x - high.astype(F32)
    mid = rest.astype(BF16)
    return high, mid, (rest - mid.astype(F32)).astype(BF16)


def gram3(x):
    h, m, l = split3(x)
    lhs = jnp.concatenate([h, h, m, h, l, m], axis=0)
    rhs = jnp.concatenate([h, m, h, l, h, m], axis=0)
    return lax.dot_general(lhs, rhs, TN_DIMS, preferred_element_type=F32)


def covariance_kernel(flags, quiet_map, seen_map, quiet_root, seen_root, init_root, out_ref, maps, maps_t, grams, cov, panel, held):
    size = out_ref.shape[0]
    total = flags.shape[0] - 1
    for index, (map_ref, root_ref) in enumerate(((quiet_map, quiet_root), (seen_map, seen_root))):
        h, l = split2(map_ref[...])
        maps[index] = jnp.concatenate([h, h, l], axis=1)
        h, l = split2(map_ref[...].T)
        maps_t[index] = jnp.concatenate([h, h, l], axis=0)
        grams[index] = gram3(root_ref[...])
    cov[...] = gram3(init_root[...])

    def advance(t, carry):
        flag = jnp.where(flags[t] > 0, 1, 0)
        h, l = split2(cov[...])
        moved = jnp.dot(maps[flag], jnp.concatenate([h, l, h], axis=0), preferred_element_type=F32)
        h, l = split2(moved)
        cov[...] = jnp.dot(jnp.concatenate([h, l, h], axis=1), maps_t[flag], preferred_element_type=F32) + grams[flag]
        return carry

    lax.fori_loop(0, flags[total], advance, 0)

    lane = lax.broadcasted_iota(jnp.int32, (8, size), 1)
    held[...] = jnp.zeros_like(held)
    panel[...] = cov[0:NB, :]

    def block(b, carry):
        start = pl.multiple_of(b * NB, NB)
        before = held[...]
        rows = panel[...]
        corner = pltpu.roll(rows, lax.rem(size - start, size), 1)[:, 0:128]
        wide = [jnp.broadcast_to(corner[:, k : k + 1], (NB, 128)) for k in range(NB)]
        d = [[None] * NB for _ in range(NB)]
        for k in range(NB):
            for i in range(k + 1):
                d[i][k] = jnp.broadcast_to(wide[k][i : i + 1, :], (8, 128))
        lines = [jnp.broadcast_to(panel[i : i + 1, :], (8, size)) for i in range(NB)]
        for j in range(NB):
            r = lax.rsqrt(d[j][j])
            r = r * (1.5 - 0.5 * d[j][j] * r * r)
            u = {k: d[j][k] * r for k in range(j + 1, NB)}
            twice = jnp.concatenate([r] * (size // 128), axis=1)
            line = jnp.where(lane >= start + j, lines[j] * twice, 0.0)
            held[j : j + 1, :] = line[0:1, :]
            for i in range(j + 1, NB):
                lines[i] = lines[i] - jnp.concatenate([u[i]] * (size // 128), axis=1) * line
                for k in range(i, NB):
                    d[i][k] = d[i][k] - u[i] * u[k]
        cov[...] = cov[...] - gram3(before)
        done = held[...]
        out_ref[pl.ds(start, NB), :] = done
        after = lax.rem(start + NB, size)
        turned = pltpu.roll(done, lax.rem(size - after, size), 1)[:, 0:128]
        h, m, l = split3(done)
        p, q, s = split3(turned)
        lhs = jnp.concatenate([p, p, q, p, s, q], axis=0)
        rhs = jnp.concatenate([h, m, h, l, h, m], axis=0)
        change = lax.dot_general(lhs, rhs, TN_DIMS, preferred_element_type=F32)
        panel[...] = cov[pl.ds(pl.multiple_of(after, NB), NB), :] - change[0:NB, :]
        return carry

    lax.fori_loop(0, size // NB, block, 0)


def covariance(flags_and_count, transition, update_map, quiet_root, observed_root, init_root):
    size = transition.shape[0]
    return pl.pallas_call(
        covariance_kernel,
        in_specs=[SMEM] + [VMEM] * 5,
        out_specs=VMEM,
        out_shape=jax.ShapeDtypeStruct((size, size), F32),
        scratch_shapes=[
            pltpu.VMEM((2, size, 3 * size), BF16),
            pltpu.VMEM((2, 3 * size, size), BF16),
            pltpu.VMEM((2, size, size), F32),
            pltpu.VMEM((size, size), F32),
            pltpu.VMEM((NB, size), F32),
            pltpu.VMEM((NB, size), F32),
        ],
        compiler_params=pltpu.CompilerParams(vmem_limit_bytes=48 * 2**20),
        cost_estimate=pl.CostEstimate(flops=2 * 200 * size**3, bytes_accessed=2**22, transcendentals=0),
    )(flags_and_count, transition, update_map, quiet_root, observed_root, init_root)


def means_kernel(flags, quiet_map, seen_map, start, shares, out_ref, maps, maps_t, shifts, columns, lines):
    steps = shares.shape[0] * shares.shape[2]
    per, width = shares.shape[2], quiet_map.shape[0]
    for index, map_ref in enumerate((quiet_map, seen_map)):
        maps[index] = map_ref[...]
        maps_t[index] = map_ref[...].T
    shifts[...] = jnp.zeros_like(shifts)
    for block in range(shares.shape[0]):
        total = shares[block, 0]
        for part in range(1, shares.shape[1]):
            total = total + shares[block, part]
        shifts[block * per : (block + 1) * per, :] = total
    columns[...] = shifts[...].T
    lines[...] = jnp.zeros_like(lines)
    lane = lax.broadcasted_iota(jnp.int32, columns.shape, 1)
    row = start[...]
    column = None
    turned = jnp.zeros(columns.shape, F32)
    for t in range(steps):
        flag = jnp.where(flags[t] > 0, 1, 0)
        if t % 2 == 0:
            column = jnp.sum(maps[flag] * row, axis=1, keepdims=True) + columns[:, t : t + 1]
            turned = jnp.where(lane == t, column, turned)
        else:
            row = jnp.sum(maps_t[flag] * column, axis=0, keepdims=True) + shifts[t : t + 1, :]
            lines[t : t + 1, :] = row
    lines[...] = lines[...] + turned.T
    for block in range(shares.shape[0]):

        @pl.when(flags[steps] == (block + 1) * per)
        def _():
            out_ref[...] = lines[block * per : (block + 1) * per, :]


def means(flags_and_count, transition, update_map, init_mean, shares):
    size = transition.shape[0]
    steps = shares.shape[0] * shares.shape[2]
    padded = -(-steps // 128) * 128
    return pl.pallas_call(
        means_kernel,
        in_specs=[SMEM] + [VMEM] * 4,
        out_specs=VMEM,
        out_shape=jax.ShapeDtypeStruct((shares.shape[2], size), F32),
        scratch_shapes=[
            pltpu.VMEM((2, size, size), F32),
            pltpu.VMEM((2, size, size), F32),
            pltpu.VMEM((padded, size), F32),
            pltpu.VMEM((size, padded), F32),
            pltpu.VMEM((padded, size), F32),
        ],
        compiler_params=pltpu.CompilerParams(vmem_limit_bytes=48 * 2**20),
    )(flags_and_count, transition, update_map, init_mean[None], shares)


def local(frames, conv_taps, pooling, gain_matrix, transition, update_map, quiet_root, observed_root, init_mean, init_root, observed):
    step_count, channels, tile_rows, width = frames.shape
    reach = DILATION_STEP
    spaces = lax.axis_size("space")
    all_flags = lax.all_gather(observed, "tm", tiled=True)
    count = ((lax.axis_index("tm") + 1) * step_count).astype(jnp.int32)
    flags_and_count = jnp.concatenate([all_flags, count[None]])
    forward = [(i, i + 1) for i in range(spaces - 1)]
    backward = [(target, source) for source, target in forward]
    low = lax.ppermute(frames[:, :, tile_rows - reach :, :], "space", forward)
    high = lax.ppermute(frames[:, :, :reach, :], "space", backward)

    spread = jnp.pad(pooling, ((2 * reach, 2 * reach), (reach, reach)))
    pools = jnp.stack([
        spread[(1 - a) * reach : (1 - a) * reach + tile_rows + 2 * reach, (1 - b) * reach : (1 - b) * reach + width]
        for a in range(-1, 2)
        for b in range(-1, 2)
    ])
    grads, sums = moments(
        frames, pools[:, reach : reach + tile_rows], conv_taps, observed,
        lambda e: e, lambda r, c: r >= 0, tile_rows,
    )
    none = jnp.zeros((step_count, channels, reach, width), frames.dtype)
    edges = jnp.concatenate(
        [low, frames[:, :, : 2 * reach], none, frames[:, :, tile_rows - 2 * reach :], high, none], axis=2
    )
    flat = jnp.zeros((9, 3 * reach, width), F32)
    edge_pools = jnp.concatenate([pools[:, :reach], flat, flat[:, : 2 * reach], pools[:, reach + tile_rows :], flat[:, :reach]], axis=1)

    def position(e):
        return jnp.where(e < 4 * reach, e - reach, e + tile_rows - 6 * reach)

    def inside(r, c):
        same = (r < 4 * reach) == (c < 4 * reach)
        real = lambda e: lax.rem(e, 4 * reach) < 3 * reach
        halo = lambda e: (position(e) < 0) | (position(e) >= tile_rows)
        return same & real(r) & real(c) & (halo(r) | halo(c))

    edge_grads, edge_sums = moments(edges, edge_pools, conv_taps, observed, position, inside, tile_rows)
    weights = observed.astype(F32)
    gain_part = jnp.dot(sums + edge_sums, gain_matrix.T, precision=lax.Precision.HIGHEST, preferred_element_type=F32)
    gain_part = gain_part * weights[:, None]
    grad_local = (grads + edge_grads) / (tile_rows * spaces * width)
    shares = lax.all_gather(gain_part, ("tm", "space", "chan"))
    shares = shares.reshape(lax.axis_size("tm"), -1, step_count, transition.shape[0])
    tap_gradient = lax.psum(grad_local, "space")[None]
    roots = covariance(flags_and_count, transition, update_map, quiet_root, observed_root, init_root)
    filtered_means = means(flags_and_count, transition, update_map, init_mean, shares)
    return (filtered_means, roots[None], tap_gradient)


def solution(mesh):
    return jax.shard_map(
        local,
        mesh=mesh,
        in_specs=(
            P(("groups", "tm"), "chan", "space", None),
            P("chan", None),
            P("space", None),
            P(None, ("space", "chan")),
            P(),
            P(),
            P(),
            P(),
            P("groups"),
            P("groups", None),
            P(("groups", "tm")),
        ),
        out_specs=(
            P(("groups", "tm"), None),
            P(("groups", "tm"), None, None),
            P(("groups", "tm"), "chan", None),
        ),
        check_vma=False,
    )
```

```python
import functools

import jax
import jax.numpy as jnp
from jax import lax
from jax.experimental import pallas as pl
from jax.experimental.pallas import tpu as pltpu
from jax.sharding import PartitionSpec as P

DILATION_STEP = 2
NB = 16
F32 = jnp.float32
BF16 = jnp.bfloat16
VMEM = pl.BlockSpec(memory_space=pltpu.VMEM)
SMEM = pl.BlockSpec(memory_space=pltpu.SMEM)

NT_DIMS = (((1,), (1,)), ((), ()))
TN_DIMS = (((0,), (0,)), ((), ()))
PAIRS = (((0, 0), 0), ((1, 1), 1), ((-1, -1), 2), ((0, 1), 3), ((-1, 0), 3), ((-1, 1), 4))


MESH = pl.DeviceIdType.MESH


def fold_grads(grads, kind, gram, rows, group, owner, row_h, col_h, allowed, limit, wide):
    folded = jnp.zeros((rows, group * rows), F32)
    for c in range(group):
        folded = jnp.where(owner == c, gram[c * rows : (c + 1) * rows, :], folded)
    for a in range(-1, 2):
        for z in range(-1, 2):
            h = row_h - DILATION_STEP * a
            keep = (h >= 0) & (h < limit) & (row_h - col_h == DILATION_STEP * (a - z)) & allowed
            row = jnp.sum(jnp.where(keep, folded, 0.0), axis=0, keepdims=True)
            for (b, y), which in PAIRS:
                if which != kind:
                    continue
                k, q = 3 * (a + 1) + b + 1, 3 * (z + 1) + y + 1
                grads[k] = grads[k] + row * wide[q]
                if b != y:
                    grads[q] = grads[q] + row * wide[k]


def gram_grads(blocks, flags, wide, rows, group, row_h, col_h, allowed, limit):
    size, width = blocks[0].shape
    reach = DILATION_STEP
    lane = lax.broadcasted_iota(jnp.int32, (size, width), 1)
    left, low, high, one, two = [], [], [], [], []
    for t, block in enumerate(blocks):
        x = block.astype(F32)
        scaled = x * flags[t]
        left.append(scaled.astype(BF16))
        low.append(jnp.where(lane >= reach, scaled, 0.0).astype(BF16))
        high.append(jnp.where(lane < width - reach, scaled, 0.0).astype(BF16))
        one.append(jnp.where(lane < width - reach, pltpu.roll(x, width - reach, 1), 0.0).astype(BF16))
        two.append(jnp.where(lane < width - 2 * reach, pltpu.roll(x, width - 2 * reach, 1), 0.0).astype(BF16))
    cat = lambda pieces: jnp.concatenate(pieces, axis=1)
    left, plain = cat(left), cat(blocks)
    owner = lax.div(lax.broadcasted_iota(jnp.int32, (rows, size), 1), rows)
    grads = [jnp.zeros((1, size), F32) for _ in range(9)]
    for kind, (lhs, rhs) in enumerate(((left, plain), (cat(low), plain), (cat(high), plain), (left, cat(one)), (left, cat(two)))):
        gram = lax.dot_general(lhs, rhs, NT_DIMS, preferred_element_type=F32)
        fold_grads(grads, kind, gram, rows, group, owner, row_h, col_h, allowed, limit, wide)
    return grads


def observe_kernel(sizes, flags, taps, x_ref, pooling, gains, shift_ref, flag_ref, grad_ref,
                   tops, bottoms, lows, highs, pools, sums, grads_all, slots, grad_slots,
                   halo_send, halo_recv, send_sem, recv_sem, grad_send, grad_recv):
    n_tm, n_space, n_chan = sizes
    steps, channels, rows, width = x_ref.shape
    reach = DILATION_STEP
    group = min(channels, 256 // rows)
    groups = channels // group
    size = group * rows
    pack = group * reach
    n_all = n_tm * n_space * n_chan
    tm, space, chan = lax.axis_index("tm"), lax.axis_index("space"), lax.axis_index("chan")
    me = (tm * n_space + space) * n_chan + chan

    def place(p):
        return {"tm": lax.div(p, n_space * n_chan), "space": lax.rem(lax.div(p, n_chan), n_space), "chan": lax.rem(p, n_chan)}

    barrier = pltpu.get_barrier_semaphore()

    def greet(i, carry):
        pl.semaphore_signal(barrier, inc=1, device_id=place(lax.rem(me + i, n_all)), device_id_type=MESH)
        return carry

    lax.fori_loop(1, n_all, greet, 0)

    def pick(count, first_row):
        r = lax.broadcasted_iota(jnp.int32, (count, size), 0)
        c = lax.broadcasted_iota(jnp.int32, (count, size), 1)
        return jnp.where(c == lax.div(r, reach) * rows + lax.rem(r, reach) + first_row, 1.0, 0.0).astype(BF16)

    pick_top, pick_bottom = pick(pack, 0), pick(pack, rows - reach)
    for t in range(steps):
        for g in range(groups):
            x = x_ref[t, g * group : (g + 1) * group].reshape(size, width)
            at = pl.ds((g * steps + t) * pack, pack)
            tops[at, :] = jnp.dot(pick_top, x, preferred_element_type=F32).astype(BF16)
            bottoms[at, :] = jnp.dot(pick_bottom, x, preferred_element_type=F32).astype(BF16)
    pl.semaphore_wait(barrier, n_all - 1)
    down = pltpu.make_async_remote_copy(
        src_ref=bottoms, dst_ref=lows, send_sem=halo_send.at[0], recv_sem=halo_recv.at[0],
        device_id={"space": lax.rem(space + 1, n_space)}, device_id_type=MESH)
    up = pltpu.make_async_remote_copy(
        src_ref=tops, dst_ref=highs, send_sem=halo_send.at[1], recv_sem=halo_recv.at[1],
        device_id={"space": lax.rem(space + n_space - 1, n_space)}, device_id_type=MESH)
    has_next, has_last = space < n_space - 1, space > 0

    @pl.when(has_next)
    def _():
        down.start()

    @pl.when(has_last)
    def _():
        up.start()

    pool = pooling[...]
    row_i = lax.broadcasted_iota(jnp.int32, (rows, width), 0)
    lane_i = lax.broadcasted_iota(jnp.int32, (rows, width), 1)
    for b in range(-1, 2):
        moved = pool
        if b:
            moved = pltpu.roll(pool, (reach * b) % width, 1)
            moved = jnp.where((lane_i >= reach * b) & (lane_i < width + reach * b), moved, 0.0)
        for a in range(-1, 2):
            turned = moved
            if a:
                turned = pltpu.roll(moved, (reach * a) % rows, 0)
                turned = jnp.where((row_i >= reach * a) & (row_i < rows + reach * a), turned, 0.0)
            pools[3 * (a + 1) + b + 1] = turned
    flag_values = [flags[t].astype(F32) for t in range(steps)]

    def widened(first, count, each):
        owner = lax.div(lax.broadcasted_iota(jnp.int32, (1, count * each), 1), each)
        wide = []
        for k in range(9):
            row = jnp.zeros((1, count * each), F32)
            for c in range(count):
                row = jnp.where(owner == c, taps[first + c, k], row)
            wide.append(row)
        return wide

    def reduced(grads, first, count, each):
        stack = jnp.concatenate(grads + [jnp.zeros((7, count * each), F32)], axis=0)
        r = lax.broadcasted_iota(jnp.int32, (count * each, 128), 0)
        c = lax.broadcasted_iota(jnp.int32, (count * each, 128), 1)
        ones = jnp.where(c == first + lax.div(r, each), 1.0, 0.0).astype(BF16)
        h, m, l = split3(stack)
        dot = lambda part: jnp.dot(part, ones, preferred_element_type=F32)
        return dot(h) + (dot(m) + dot(l))

    grads_all[...] = jnp.zeros_like(grads_all)
    row_e = lax.broadcasted_iota(jnp.int32, (rows, size), 0)
    col_e = lax.rem(lax.broadcasted_iota(jnp.int32, (rows, size), 1), rows)

    def interior(g, carry):
        first = g * group
        for c in range(group):
            weight = taps[first + c, 0] * pools[0]
            for k in range(1, 9):
                weight = weight + taps[first + c, k] * pools[k]
            for t in range(steps):
                part = x_ref[t, first + c].astype(F32) * weight
                sums[t, pl.ds(first + c, 1), :] = jnp.sum(part, axis=0, keepdims=True)
        blocks = [x_ref[t, pl.ds(first, group)].reshape(size, width) for t in range(steps)]
        grads = gram_grads(blocks, flag_values, widened(first, group, rows), rows, group, row_e, col_e, row_e >= 0, rows)
        grads_all[...] += reduced(grads, first, group, rows)
        return carry

    lax.fori_loop(0, groups, interior, 0)

    @pl.when(has_last)
    def _():
        up.wait_send()
        down.wait_recv()

    @pl.when(has_next)
    def _():
        down.wait_send()
        up.wait_recv()

    edge = 8 * reach
    half = group * edge
    r = lax.broadcasted_iota(jnp.int32, (half, size), 0)
    c = lax.broadcasted_iota(jnp.int32, (half, size), 1)
    e = lax.rem(r, edge)

    def position(e):
        return jnp.where(e < 4 * reach, e - reach, e + rows - 6 * reach)

    def real(e):
        return lax.rem(e, 4 * reach) < 3 * reach

    def halo(e):
        return (position(e) < 0) | (position(e) >= rows)

    own = jnp.where(real(e) & ~halo(e) & (c == lax.div(r, edge) * rows + position(e)), 1.0, 0.0).astype(BF16)
    r = lax.broadcasted_iota(jnp.int32, (half, pack), 0)
    c = lax.broadcasted_iota(jnp.int32, (half, pack), 1)
    e = lax.rem(r, edge)
    from_low = jnp.where((e < reach) & (c == lax.div(r, edge) * reach + e), 1.0, 0.0).astype(BF16)
    from_high = jnp.where((e >= 6 * reach) & (e < 7 * reach) & (c == lax.div(r, edge) * reach + e - 6 * reach), 1.0, 0.0).astype(BF16)
    edge_row = lax.broadcasted_iota(jnp.int32, (edge, width), 0)
    edge_pools = []
    for b in range(3):
        shifted = pools[3 + b]
        low_part = jnp.where(edge_row < reach, shifted[0:edge, :], 0.0)
        high_part = jnp.where((edge_row >= 6 * reach) & (edge_row < 7 * reach), pltpu.roll(shifted[rows - edge : rows, :], edge - reach, 0), 0.0)
        edge_pools.append((low_part, high_part))
    many = 2 * group
    e_row = lax.broadcasted_iota(jnp.int32, (edge, many * edge), 0)
    e_col = lax.rem(lax.broadcasted_iota(jnp.int32, (edge, many * edge), 1), edge)
    allowed = ((e_row < 4 * reach) == (e_col < 4 * reach)) & real(e_row) & real(e_col) & (halo(e_row) | halo(e_col))

    def outer(v, carry):
        blocks = []
        for t in range(steps):
            halves = []
            for q in range(2):
                g = 2 * v + q
                x = x_ref[t, pl.ds(g * group, group)].reshape(size, width)
                at = pl.ds(pl.multiple_of((g * steps + t) * pack, pack), pack)
                low_rows = jnp.where(has_last, lows[at, :].astype(F32), 0.0).astype(BF16)
                high_rows = jnp.where(has_next, highs[at, :].astype(F32), 0.0).astype(BF16)
                dot = lambda m, y: jnp.dot(m, y, preferred_element_type=F32)
                halves.append(dot(own, x) + dot(from_low, low_rows) + dot(from_high, high_rows))
            blocks.append(jnp.concatenate(halves, axis=0))
        first = v * many
        for i in range(many):
            weight = jnp.zeros((edge, width), F32)
            for b in range(3):
                low_part, high_part = edge_pools[b]
                weight = weight + taps[first + i, b] * low_part + taps[first + i, 6 + b] * high_part
            for t in range(steps):
                part = blocks[t][i * edge : (i + 1) * edge, :] * weight
                at = pl.ds(first + i, 1)
                sums[t, at, :] = sums[t, at, :] + jnp.sum(part, axis=0, keepdims=True)
        grads = gram_grads([y.astype(BF16) for y in blocks], flag_values, widened(first, many, edge), edge, many, position(e_row), position(e_col), allowed, rows)
        grads_all[...] += reduced(grads, first, many, edge)
        return carry

    lax.fori_loop(0, groups // 2, outer, 0)

    scale = 1.0 / (rows * n_space * width)
    grad_slots[space] = grads_all[...] * scale
    for t in range(steps):
        tile = jnp.sum(sums[t], axis=1, keepdims=True)
        share = jnp.sum(tile * gains[...], axis=0, keepdims=True) * flag_values[t]
        slots[me, pl.ds(t, 1), :] = share
        slots[me, pl.ds(steps + t, 1), :] = jnp.zeros((1, share.shape[1]), F32) + flag_values[t]

    def share_copy(p, slot):
        return pltpu.make_async_remote_copy(
            src_ref=slots.at[slot], dst_ref=slots.at[slot], send_sem=send_sem.at[p], recv_sem=recv_sem.at[slot],
            device_id=place(p), device_id_type=MESH)

    def grad_copy(s, slot):
        return pltpu.make_async_remote_copy(
            src_ref=grad_slots.at[slot], dst_ref=grad_slots.at[slot], send_sem=grad_send.at[s], recv_sem=grad_recv.at[slot],
            device_id={"space": s}, device_id_type=MESH)

    def each(count, mine, act):
        def turn(i, carry):
            act(lax.rem(mine + i, count))
            return carry

        lax.fori_loop(1, count, turn, 0)

    each(n_all, me, lambda p: share_copy(p, me).start())
    each(n_space, space, lambda s: grad_copy(s, space).start())
    each(n_all, me, lambda p: share_copy(p, p).wait_recv())
    each(n_space, space, lambda s: grad_copy(s, s).wait_recv())
    for block in range(n_tm):
        total = slots[block * n_space * n_chan, 0:steps, :]
        for part in range(1, n_space * n_chan):
            total = total + slots[block * n_space * n_chan + part, 0:steps, :]
        shift_ref[block * steps : (block + 1) * steps, :] = total
        marks = slots[block * n_space * n_chan, steps : 2 * steps, 0:128]
        flag_ref[block * steps : (block + 1) * steps, :] = jnp.where(marks > 0.5, 1, 0)
    total = grad_slots[0]
    for part in range(1, n_space):
        total = total + grad_slots[part]
    grad_ref[...] = total[0:9, 0:channels]
    each(n_all, me, lambda p: share_copy(p, me).wait_send())
    each(n_space, space, lambda s: grad_copy(s, space).wait_send())


def observe(flags, taps, frames, pooling, gains):
    steps, channels, rows, width = frames.shape
    states = gains.shape[1]
    sizes = tuple(lax.axis_size(name) for name in ("tm", "space", "chan"))
    n_all = sizes[0] * sizes[1] * sizes[2]
    packed = steps * channels * DILATION_STEP
    return pl.pallas_call(
        functools.partial(observe_kernel, sizes),
        in_specs=[SMEM, SMEM, VMEM, VMEM, VMEM],
        out_specs=[VMEM] * 3,
        out_shape=[
            jax.ShapeDtypeStruct((sizes[0] * steps, states), F32),
            jax.ShapeDtypeStruct((sizes[0] * steps, 128), jnp.int32),
            jax.ShapeDtypeStruct((9, channels), F32),
        ],
        scratch_shapes=[pltpu.VMEM((packed, width), BF16)] * 4 + [
            pltpu.VMEM((9, rows, width), F32),
            pltpu.VMEM((steps, channels, width), F32),
            pltpu.VMEM((16, 128), F32),
            pltpu.VMEM((n_all, 2 * steps, states), F32),
            pltpu.VMEM((sizes[1], 16, 128), F32),
            pltpu.SemaphoreType.DMA((2,)),
            pltpu.SemaphoreType.DMA((2,)),
            pltpu.SemaphoreType.DMA((n_all,)),
            pltpu.SemaphoreType.DMA((n_all,)),
            pltpu.SemaphoreType.DMA((sizes[1],)),
            pltpu.SemaphoreType.DMA((sizes[1],)),
        ],
        compiler_params=pltpu.CompilerParams(collective_id=0, has_side_effects=True, vmem_limit_bytes=48 * 2**20),
    )(flags, taps, frames, pooling, gains)


def split2(x):
    high = x.astype(BF16)
    return high, (x - high.astype(F32)).astype(BF16)


def split3(x):
    high = x.astype(BF16)
    rest = x - high.astype(F32)
    mid = rest.astype(BF16)
    return high, mid, (rest - mid.astype(F32)).astype(BF16)


def gram3(x):
    h, m, l = split3(x)
    lhs = jnp.concatenate([h, h, m, h, l, m], axis=0)
    rhs = jnp.concatenate([h, m, h, l, h, m], axis=0)
    return lax.dot_general(lhs, rhs, TN_DIMS, preferred_element_type=F32)


def mean_chain(per, tm, flags, quiet_map, seen_map, start, shift_ref, out_ref, maps, maps_t, shifts, columns, lines):
    steps = shift_ref.shape[0]
    for index, map_ref in enumerate((quiet_map, seen_map)):
        maps[index] = map_ref[...]
        maps_t[index] = map_ref[...].T
    shifts[...] = jnp.zeros_like(shifts)
    shifts[0:steps, :] = shift_ref[...]
    columns[...] = shifts[...].T
    lines[...] = jnp.zeros_like(lines)
    lane = lax.broadcasted_iota(jnp.int32, columns.shape, 1)
    row = start[...]
    column = None
    turned = jnp.zeros(columns.shape, F32)
    for t in range(steps):
        flag = flags[t, 0]
        if t % 2 == 0:
            column = jnp.sum(maps[flag] * row, axis=1, keepdims=True) + columns[:, t : t + 1]
            turned = jnp.where(lane == t, column, turned)
        else:
            row = jnp.sum(maps_t[flag] * column, axis=0, keepdims=True) + shifts[t : t + 1, :]
            lines[t : t + 1, :] = row
    lines[...] = lines[...] + turned.T
    for block in range(steps // per):

        @pl.when(tm == block)
        def _():
            out_ref[...] = lines[block * per : (block + 1) * per, :]


def state_kernel(per, flags, quiet_map, seen_map, quiet_root, seen_root, init_root, start_mean, shift_ref, out_ref, mean_ref, maps, maps_t, grams, cov, panel, held, plain, plain_t, shifts, columns, lines):
    size = out_ref.shape[0]
    tm = lax.axis_index("tm")
    mean_chain(per, tm, flags, quiet_map, seen_map, start_mean, shift_ref, mean_ref, plain, plain_t, shifts, columns, lines)
    for index, (map_ref, root_ref) in enumerate(((quiet_map, quiet_root), (seen_map, seen_root))):
        h, l = split2(map_ref[...])
        maps[index] = jnp.concatenate([h, h, l], axis=1)
        h, l = split2(map_ref[...].T)
        maps_t[index] = jnp.concatenate([h, h, l], axis=0)
        grams[index] = gram3(root_ref[...])
    cov[...] = gram3(init_root[...])

    def advance(t, carry):
        flag = flags[t, 0]
        h, l = split2(cov[...])
        moved = jnp.dot(maps[flag], jnp.concatenate([h, l, h], axis=0), preferred_element_type=F32)
        h, l = split2(moved)
        cov[...] = jnp.dot(jnp.concatenate([h, l, h], axis=1), maps_t[flag], preferred_element_type=F32) + grams[flag]
        return carry

    lax.fori_loop(0, (tm + 1) * per, advance, 0)

    lane = lax.broadcasted_iota(jnp.int32, (8, size), 1)
    held[...] = jnp.zeros_like(held)
    panel[...] = cov[0:NB, :]

    def block(b, carry):
        start = pl.multiple_of(b * NB, NB)
        before = held[...]
        rows = panel[...]
        corner = pltpu.roll(rows, lax.rem(size - start, size), 1)[:, 0:128]
        wide = [jnp.broadcast_to(corner[:, k : k + 1], (NB, 128)) for k in range(NB)]
        d = [[None] * NB for _ in range(NB)]
        for k in range(NB):
            for i in range(k + 1):
                d[i][k] = jnp.broadcast_to(wide[k][i : i + 1, :], (8, 128))
        lines = [jnp.broadcast_to(panel[i : i + 1, :], (8, size)) for i in range(NB)]
        for j in range(NB):
            r = lax.rsqrt(d[j][j])
            r = r * (1.5 - 0.5 * d[j][j] * r * r)
            u = {k: d[j][k] * r for k in range(j + 1, NB)}
            twice = jnp.concatenate([r] * (size // 128), axis=1)
            line = jnp.where(lane >= start + j, lines[j] * twice, 0.0)
            held[j : j + 1, :] = line[0:1, :]
            for i in range(j + 1, NB):
                lines[i] = lines[i] - jnp.concatenate([u[i]] * (size // 128), axis=1) * line
                for k in range(i, NB):
                    d[i][k] = d[i][k] - u[i] * u[k]
        cov[...] = cov[...] - gram3(before)
        done = held[...]
        out_ref[pl.ds(start, NB), :] = done
        after = lax.rem(start + NB, size)
        turned = pltpu.roll(done, lax.rem(size - after, size), 1)[:, 0:128]
        h, m, l = split3(done)
        p, q, s = split3(turned)
        lhs = jnp.concatenate([p, p, q, p, s, q], axis=0)
        rhs = jnp.concatenate([h, m, h, l, h, m], axis=0)
        change = lax.dot_general(lhs, rhs, TN_DIMS, preferred_element_type=F32)
        panel[...] = cov[pl.ds(pl.multiple_of(after, NB), NB), :] - change[0:NB, :]
        return carry

    lax.fori_loop(0, size // NB, block, 0)


def state(per, flags, transition, update_map, quiet_root, observed_root, init_root, init_mean, shifts):
    size = transition.shape[0]
    steps = shifts.shape[0]
    padded = -(-steps // 128) * 128
    return pl.pallas_call(
        functools.partial(state_kernel, per),
        in_specs=[SMEM] + [VMEM] * 7,
        out_specs=[VMEM] * 2,
        out_shape=[jax.ShapeDtypeStruct((size, size), F32), jax.ShapeDtypeStruct((per, size), F32)],
        scratch_shapes=[
            pltpu.VMEM((2, size, 3 * size), BF16),
            pltpu.VMEM((2, 3 * size, size), BF16),
            pltpu.VMEM((2, size, size), F32),
            pltpu.VMEM((size, size), F32),
            pltpu.VMEM((NB, size), F32),
            pltpu.VMEM((NB, size), F32),
            pltpu.VMEM((2, size, size), F32),
            pltpu.VMEM((2, size, size), F32),
            pltpu.VMEM((padded, size), F32),
            pltpu.VMEM((size, padded), F32),
            pltpu.VMEM((padded, size), F32),
        ],
        compiler_params=pltpu.CompilerParams(vmem_limit_bytes=48 * 2**20),
    )(flags, transition, update_map, quiet_root, observed_root, init_root, init_mean[None], shifts)


def local(frames, conv_taps, pooling, gain_matrix, transition, update_map, quiet_root, observed_root, init_mean, init_root, observed):
    per = frames.shape[0]
    shifts, flags, tap_gradient = observe(observed, conv_taps, frames, pooling, gain_matrix.T)
    roots, filtered_means = state(per, flags, transition, update_map, quiet_root, observed_root, init_root, init_mean, shifts)
    return (filtered_means, roots[None], tap_gradient.T[None])


def solution(mesh):
    return jax.shard_map(
        local,
        mesh=mesh,
        in_specs=(
            P(("groups", "tm"), "chan", "space", None),
            P("chan", None),
            P("space", None),
            P(None, ("space", "chan")),
            P(),
            P(),
            P(),
            P(),
            P("groups"),
            P("groups", None),
            P(("groups", "tm")),
        ),
        out_specs=(
            P(("groups", "tm"), None),
            P(("groups", "tm"), None, None),
            P(("groups", "tm"), "chan", None),
        ),
        check_vma=False,
    )
```

```python
import functools

import jax
import jax.numpy as jnp
from jax import lax
from jax.experimental import pallas as pl
from jax.experimental.pallas import tpu as pltpu
from jax.sharding import PartitionSpec as P

DILATION_STEP = 2
NB = 16
F32 = jnp.float32
BF16 = jnp.bfloat16
VMEM = pl.BlockSpec(memory_space=pltpu.VMEM)
SMEM = pl.BlockSpec(memory_space=pltpu.SMEM)

NT_DIMS = (((1,), (1,)), ((), ()))
TN_DIMS = (((0,), (0,)), ((), ()))
PAIRS = (((0, 0), 0), ((1, 1), 1), ((-1, -1), 2), ((0, 1), 3), ((-1, 0), 3), ((-1, 1), 4))


MESH = pl.DeviceIdType.MESH


def fold_grads(grads, kind, gram, rows, group, owner, row_h, col_h, allowed, limit, wide):
    folded = jnp.zeros((rows, group * rows), F32)
    for c in range(group):
        folded = jnp.where(owner == c, gram[c * rows : (c + 1) * rows, :], folded)
    for a in range(-1, 2):
        for z in range(-1, 2):
            h = row_h - DILATION_STEP * a
            keep = (h >= 0) & (h < limit) & (row_h - col_h == DILATION_STEP * (a - z)) & allowed
            row = jnp.sum(jnp.where(keep, folded, 0.0), axis=0, keepdims=True)
            for (b, y), which in PAIRS:
                if which != kind:
                    continue
                k, q = 3 * (a + 1) + b + 1, 3 * (z + 1) + y + 1
                grads[k] = grads[k] + row * wide[q]
                if b != y:
                    grads[q] = grads[q] + row * wide[k]


def gram_grads(blocks, flags, wide, rows, group, row_h, col_h, allowed, limit):
    size, width = blocks[0].shape
    reach = DILATION_STEP
    lane = lax.broadcasted_iota(jnp.int32, (size, width), 1)
    left, low, high, one, two = [], [], [], [], []
    for t, block in enumerate(blocks):
        x = block.astype(F32)
        scaled = x * flags[t]
        left.append(scaled.astype(BF16))
        low.append(jnp.where(lane >= reach, scaled, 0.0).astype(BF16))
        high.append(jnp.where(lane < width - reach, scaled, 0.0).astype(BF16))
        one.append(jnp.where(lane < width - reach, pltpu.roll(x, width - reach, 1), 0.0).astype(BF16))
        two.append(jnp.where(lane < width - 2 * reach, pltpu.roll(x, width - 2 * reach, 1), 0.0).astype(BF16))
    cat = lambda pieces: jnp.concatenate(pieces, axis=1)
    left, plain = cat(left), cat(blocks)
    owner = lax.div(lax.broadcasted_iota(jnp.int32, (rows, size), 1), rows)
    grads = [jnp.zeros((1, size), F32) for _ in range(9)]
    for kind, (lhs, rhs) in enumerate(((left, plain), (cat(low), plain), (cat(high), plain), (left, cat(one)), (left, cat(two)))):
        gram = lax.dot_general(lhs, rhs, NT_DIMS, preferred_element_type=F32)
        fold_grads(grads, kind, gram, rows, group, owner, row_h, col_h, allowed, limit, wide)
    return grads


def observe_kernel(sizes, flags, taps, x_ref, pooling, gains, quiet_map, seen_map, quiet_root, seen_root, init_root,
                   shift_ref, flag_ref, grad_ref, cov,
                   tops, bottoms, lows, highs, pools, sums, grads_all, slots, grad_slots, flag_slots, maps, maps_t, grams,
                   halo_send, halo_recv, send_sem, recv_sem, grad_send, grad_recv, flag_send, flag_recv):
    n_tm, n_space, n_chan = sizes
    steps, channels, rows, width = x_ref.shape
    reach = DILATION_STEP
    group = min(channels, 256 // rows)
    groups = channels // group
    size = group * rows
    pack = group * reach
    n_all = n_tm * n_space * n_chan
    tm, space, chan = lax.axis_index("tm"), lax.axis_index("space"), lax.axis_index("chan")
    me = (tm * n_space + space) * n_chan + chan

    def place(p):
        return {"tm": lax.div(p, n_space * n_chan), "space": lax.rem(lax.div(p, n_chan), n_space), "chan": lax.rem(p, n_chan)}

    barrier = pltpu.get_barrier_semaphore()

    def greet(i, carry):
        pl.semaphore_signal(barrier, inc=1, device_id=place(lax.rem(me + i, n_all)), device_id_type=MESH)
        return carry

    lax.fori_loop(1, n_all, greet, 0)

    def pick(count, first_row):
        r = lax.broadcasted_iota(jnp.int32, (count, size), 0)
        c = lax.broadcasted_iota(jnp.int32, (count, size), 1)
        return jnp.where(c == lax.div(r, reach) * rows + lax.rem(r, reach) + first_row, 1.0, 0.0).astype(BF16)

    pick_top, pick_bottom = pick(pack, 0), pick(pack, rows - reach)
    for t in range(steps):
        for g in range(groups):
            x = x_ref[t, g * group : (g + 1) * group].reshape(size, width)
            at = pl.ds((g * steps + t) * pack, pack)
            tops[at, :] = jnp.dot(pick_top, x, preferred_element_type=F32).astype(BF16)
            bottoms[at, :] = jnp.dot(pick_bottom, x, preferred_element_type=F32).astype(BF16)
    prepare_chain(steps, quiet_map, seen_map, quiet_root, seen_root, init_root, maps, maps_t, grams, cov)
    for t in range(steps):
        flag_slots[tm, t : t + 1, :] = jnp.zeros((1, 128), F32) + flags[t].astype(F32)
    pl.semaphore_wait(barrier, n_all - 1)
    down = pltpu.make_async_remote_copy(
        src_ref=bottoms, dst_ref=lows, send_sem=halo_send.at[0], recv_sem=halo_recv.at[0],
        device_id={"space": lax.rem(space + 1, n_space)}, device_id_type=MESH)
    up = pltpu.make_async_remote_copy(
        src_ref=tops, dst_ref=highs, send_sem=halo_send.at[1], recv_sem=halo_recv.at[1],
        device_id={"space": lax.rem(space + n_space - 1, n_space)}, device_id_type=MESH)
    has_next, has_last = space < n_space - 1, space > 0

    @pl.when(has_next)
    def _():
        down.start()

    @pl.when(has_last)
    def _():
        up.start()

    def flag_copy(p, slot):
        return pltpu.make_async_remote_copy(
            src_ref=flag_slots.at[slot], dst_ref=flag_slots.at[slot], send_sem=flag_send.at[p], recv_sem=flag_recv.at[slot],
            device_id={"tm": p}, device_id_type=MESH)

    def each(count, mine, act):
        def turn(i, carry):
            act(lax.rem(mine + i, count))
            return carry

        lax.fori_loop(1, count, turn, 0)

    each(n_tm, tm, lambda p: flag_copy(p, tm).start())

    pool = pooling[...]
    row_i = lax.broadcasted_iota(jnp.int32, (rows, width), 0)
    lane_i = lax.broadcasted_iota(jnp.int32, (rows, width), 1)
    for b in range(-1, 2):
        moved = pool
        if b:
            moved = pltpu.roll(pool, (reach * b) % width, 1)
            moved = jnp.where((lane_i >= reach * b) & (lane_i < width + reach * b), moved, 0.0)
        for a in range(-1, 2):
            turned = moved
            if a:
                turned = pltpu.roll(moved, (reach * a) % rows, 0)
                turned = jnp.where((row_i >= reach * a) & (row_i < rows + reach * a), turned, 0.0)
            pools[3 * (a + 1) + b + 1] = turned
    flag_values = [flags[t].astype(F32) for t in range(steps)]

    def widened(first, count, each):
        owner = lax.div(lax.broadcasted_iota(jnp.int32, (1, count * each), 1), each)
        wide = []
        for k in range(9):
            row = jnp.zeros((1, count * each), F32)
            for c in range(count):
                row = jnp.where(owner == c, taps[k, first + c], row)
            wide.append(row)
        return wide

    def reduced(grads, first, count, each):
        stack = jnp.concatenate(grads + [jnp.zeros((7, count * each), F32)], axis=0)
        r = lax.broadcasted_iota(jnp.int32, (count * each, 128), 0)
        c = lax.broadcasted_iota(jnp.int32, (count * each, 128), 1)
        ones = jnp.where(c == first + lax.div(r, each), 1.0, 0.0).astype(BF16)
        h, m, l = split3(stack)
        dot = lambda part: jnp.dot(part, ones, preferred_element_type=F32)
        return dot(h) + (dot(m) + dot(l))

    grads_all[...] = jnp.zeros_like(grads_all)
    row_e = lax.broadcasted_iota(jnp.int32, (rows, size), 0)
    col_e = lax.rem(lax.broadcasted_iota(jnp.int32, (rows, size), 1), rows)

    def interior(g, carry):
        first = g * group
        for c in range(group):
            weight = taps[0, first + c] * pools[0]
            for k in range(1, 9):
                weight = weight + taps[k, first + c] * pools[k]
            for t in range(steps):
                part = x_ref[t, first + c].astype(F32) * weight
                sums[t, pl.ds(first + c, 1), :] = jnp.sum(part, axis=0, keepdims=True)
        blocks = [x_ref[t, pl.ds(first, group)].reshape(size, width) for t in range(steps)]
        grads = gram_grads(blocks, flag_values, widened(first, group, rows), rows, group, row_e, col_e, row_e >= 0, rows)
        grads_all[...] += reduced(grads, first, group, rows)
        return carry

    lax.fori_loop(0, groups, interior, 0)

    @pl.when(has_last)
    def _():
        up.wait_send()
        down.wait_recv()

    @pl.when(has_next)
    def _():
        down.wait_send()
        up.wait_recv()

    edge = 8 * reach
    half = group * edge
    r = lax.broadcasted_iota(jnp.int32, (half, size), 0)
    c = lax.broadcasted_iota(jnp.int32, (half, size), 1)
    e = lax.rem(r, edge)

    def position(e):
        return jnp.where(e < 4 * reach, e - reach, e + rows - 6 * reach)

    def real(e):
        return lax.rem(e, 4 * reach) < 3 * reach

    def halo(e):
        return (position(e) < 0) | (position(e) >= rows)

    own = jnp.where(real(e) & ~halo(e) & (c == lax.div(r, edge) * rows + position(e)), 1.0, 0.0).astype(BF16)
    r = lax.broadcasted_iota(jnp.int32, (half, pack), 0)
    c = lax.broadcasted_iota(jnp.int32, (half, pack), 1)
    e = lax.rem(r, edge)
    from_low = jnp.where((e < reach) & (c == lax.div(r, edge) * reach + e), 1.0, 0.0).astype(BF16)
    from_high = jnp.where((e >= 6 * reach) & (e < 7 * reach) & (c == lax.div(r, edge) * reach + e - 6 * reach), 1.0, 0.0).astype(BF16)
    edge_row = lax.broadcasted_iota(jnp.int32, (edge, width), 0)
    edge_pools = []
    for b in range(3):
        shifted = pools[3 + b]
        low_part = jnp.where(edge_row < reach, shifted[0:edge, :], 0.0)
        high_part = jnp.where((edge_row >= 6 * reach) & (edge_row < 7 * reach), pltpu.roll(shifted[rows - edge : rows, :], edge - reach, 0), 0.0)
        edge_pools.append((low_part, high_part))
    many = 2 * group
    e_row = lax.broadcasted_iota(jnp.int32, (edge, many * edge), 0)
    e_col = lax.rem(lax.broadcasted_iota(jnp.int32, (edge, many * edge), 1), edge)
    allowed = ((e_row < 4 * reach) == (e_col < 4 * reach)) & real(e_row) & real(e_col) & (halo(e_row) | halo(e_col))

    def outer(v, carry):
        blocks = []
        for t in range(steps):
            halves = []
            for q in range(2):
                g = 2 * v + q
                x = x_ref[t, pl.ds(g * group, group)].reshape(size, width)
                at = pl.ds(pl.multiple_of((g * steps + t) * pack, pack), pack)
                low_rows = jnp.where(has_last, lows[at, :].astype(F32), 0.0).astype(BF16)
                high_rows = jnp.where(has_next, highs[at, :].astype(F32), 0.0).astype(BF16)
                dot = lambda m, y: jnp.dot(m, y, preferred_element_type=F32)
                halves.append(dot(own, x) + dot(from_low, low_rows) + dot(from_high, high_rows))
            blocks.append(jnp.concatenate(halves, axis=0))
        first = v * many
        for i in range(many):
            weight = jnp.zeros((edge, width), F32)
            for b in range(3):
                low_part, high_part = edge_pools[b]
                weight = weight + taps[b, first + i] * low_part + taps[6 + b, first + i] * high_part
            for t in range(steps):
                part = blocks[t][i * edge : (i + 1) * edge, :] * weight
                at = pl.ds(first + i, 1)
                sums[t, at, :] = sums[t, at, :] + jnp.sum(part, axis=0, keepdims=True)
        grads = gram_grads([y.astype(BF16) for y in blocks], flag_values, widened(first, many, edge), edge, many, position(e_row), position(e_col), allowed, rows)
        grads_all[...] += reduced(grads, first, many, edge)
        return carry

    lax.fori_loop(0, groups // 2, outer, 0)

    scale = 1.0 / (rows * n_space * width)
    grad_slots[space] = grads_all[...] * scale
    for t in range(steps):
        tile = jnp.sum(sums[t], axis=1, keepdims=True)
        share = jnp.sum(tile * gains[...], axis=0, keepdims=True) * flag_values[t]
        slots[me, pl.ds(t, 1), :] = share

    def share_copy(p, slot):
        return pltpu.make_async_remote_copy(
            src_ref=slots.at[slot], dst_ref=slots.at[slot], send_sem=send_sem.at[p], recv_sem=recv_sem.at[slot],
            device_id=place(p), device_id_type=MESH)

    def grad_copy(s, slot):
        return pltpu.make_async_remote_copy(
            src_ref=grad_slots.at[slot], dst_ref=grad_slots.at[slot], send_sem=grad_send.at[s], recv_sem=grad_recv.at[slot],
            device_id={"space": s}, device_id_type=MESH)

    each(n_all, me, lambda p: share_copy(p, me).start())
    each(n_space, space, lambda s: grad_copy(s, space).start())
    each(n_tm, tm, lambda p: flag_copy(p, p).wait_recv())
    for block in range(n_tm):
        for t in range(steps):
            flag_ref[block * steps + t : block * steps + t + 1, :] = jnp.where(flag_slots[block, t : t + 1, :] > 0.5, 1, 0)
    run_chain(steps, tm, flag_ref, maps, maps_t, grams, cov)
    each(n_all, me, lambda p: share_copy(p, p).wait_recv())
    each(n_space, space, lambda s: grad_copy(s, s).wait_recv())
    for block in range(n_tm):
        total = slots[block * n_space * n_chan, 0:steps, :]
        for part in range(1, n_space * n_chan):
            total = total + slots[block * n_space * n_chan + part, 0:steps, :]
        shift_ref[block * steps : (block + 1) * steps, :] = total
    total = grad_slots[0]
    for part in range(1, n_space):
        total = total + grad_slots[part]
    grad_ref[...] = total[0:9, 0:channels]
    each(n_all, me, lambda p: share_copy(p, me).wait_send())
    each(n_space, space, lambda s: grad_copy(s, space).wait_send())
    each(n_tm, tm, lambda p: flag_copy(p, tm).wait_send())


def observe(flags, taps, frames, pooling, gains, transition, update_map, quiet_root, observed_root, init_root):
    steps, channels, rows, width = frames.shape
    states = gains.shape[1]
    sizes = tuple(lax.axis_size(name) for name in ("tm", "space", "chan"))
    n_all = sizes[0] * sizes[1] * sizes[2]
    packed = steps * channels * DILATION_STEP
    choices = 4 if steps % 2 == 0 else 2
    return pl.pallas_call(
        functools.partial(observe_kernel, sizes),
        in_specs=[SMEM, SMEM] + [VMEM] * 8,
        out_specs=[VMEM] * 4,
        out_shape=[
            jax.ShapeDtypeStruct((sizes[0] * steps, states), F32),
            jax.ShapeDtypeStruct((sizes[0] * steps, 128), jnp.int32),
            jax.ShapeDtypeStruct((9, channels), F32),
            jax.ShapeDtypeStruct((states, states), F32),
        ],
        scratch_shapes=[pltpu.VMEM((packed, width), BF16)] * 4 + [
            pltpu.VMEM((9, rows, width), F32),
            pltpu.VMEM((steps, channels, width), F32),
            pltpu.VMEM((16, 128), F32),
            pltpu.VMEM((n_all, 8 * (-(-steps // 8)), states), F32),
            pltpu.VMEM((sizes[1], 16, 128), F32),
            pltpu.VMEM((sizes[0], 8 * (-(-steps // 8)), 128), F32),
            pltpu.VMEM((choices, states, 3 * states), BF16),
            pltpu.VMEM((choices, 3 * states, states), BF16),
            pltpu.VMEM((choices, states, states), F32),
            pltpu.SemaphoreType.DMA((2,)),
            pltpu.SemaphoreType.DMA((2,)),
            pltpu.SemaphoreType.DMA((n_all,)),
            pltpu.SemaphoreType.DMA((n_all,)),
            pltpu.SemaphoreType.DMA((sizes[1],)),
            pltpu.SemaphoreType.DMA((sizes[1],)),
            pltpu.SemaphoreType.DMA((sizes[0],)),
            pltpu.SemaphoreType.DMA((sizes[0],)),
        ],
        compiler_params=pltpu.CompilerParams(collective_id=0, has_side_effects=True, vmem_limit_bytes=60 * 2**20),
    )(flags, taps, frames, pooling, gains, transition, update_map, quiet_root, observed_root, init_root)


def split2(x):
    high = x.astype(BF16)
    return high, (x - high.astype(F32)).astype(BF16)


def split3(x):
    high = x.astype(BF16)
    rest = x - high.astype(F32)
    mid = rest.astype(BF16)
    return high, mid, (rest - mid.astype(F32)).astype(BF16)


def gram3(x):
    h, m, l = split3(x)
    lhs = jnp.concatenate([h, h, m, h, l, m], axis=0)
    rhs = jnp.concatenate([h, m, h, l, h, m], axis=0)
    return lax.dot_general(lhs, rhs, TN_DIMS, preferred_element_type=F32)


def left_form(x):
    h, l = split2(x)
    return jnp.concatenate([h, h, l], axis=1)


def right_form(x):
    h, l = split2(x)
    return jnp.concatenate([h, l, h], axis=0)


def right_map(x):
    h, l = split2(x)
    return jnp.concatenate([h, h, l], axis=0)


def left_moving(x):
    h, l = split2(x)
    return jnp.concatenate([h, l, h], axis=1)


def product(lhs, rhs):
    return jnp.dot(lhs, rhs, preferred_element_type=F32)


def prepare_chain(steps, quiet_map, seen_map, quiet_root, seen_root, init_root, maps, maps_t, grams, cov):
    cov[...] = gram3(init_root[...])
    grams[0], grams[1] = gram3(quiet_root[...]), gram3(seen_root[...])
    single = [(quiet_map[...], grams[0]), (seen_map[...], grams[1])]
    if steps % 2:
        joined = single
    else:
        joined = []
        for index, (later, noise) in enumerate(single):
            lhs = left_form(later)
            maps_t[index] = right_map(later.T)
            rhs = maps_t[index]
            for earlier, earlier_noise in single:
                moved = product(lhs, right_form(earlier_noise))
                joined.append((product(lhs, right_form(earlier)), product(left_moving(moved), rhs) + noise))
    for index, (both, noise) in enumerate(joined):
        maps[index] = left_form(both)
        maps_t[index] = right_map(both.T)
        grams[index] = noise


def run_chain(steps, tm, flag_ref, maps, maps_t, grams, cov):
    paired = steps % 2 == 0

    def advance(t, carry):
        if paired:
            which = 2 * flag_ref[2 * t + 1, 0] + flag_ref[2 * t, 0]
        else:
            which = flag_ref[t, 0]
        moved = product(maps[which], right_form(cov[...]))
        cov[...] = product(left_moving(moved), maps_t[which]) + grams[which]
        return carry

    lax.fori_loop(0, (tm + 1) * (steps // 2 if paired else steps), advance, 0)


def state_kernel(per, flags, cov_ref, quiet_map, seen_map, start_mean, shift_ref, grad_in, out_ref, mean_ref, grad_ref,
                 cov, panel, held, plain, plain_t, shifts, columns, lines, turned):
    size = out_ref.shape[0]
    steps = shift_ref.shape[0]
    tm = lax.axis_index("tm")
    grad_ref[...] = grad_in[...]
    for index, map_ref in enumerate((quiet_map, seen_map)):
        plain[index] = map_ref[...]
        plain_t[index] = map_ref[...].T
    shifts[...] = jnp.zeros_like(shifts)
    shifts[0:steps, :] = shift_ref[...]
    columns[...] = shifts[...].T
    lines[...] = jnp.zeros_like(lines)
    turned[...] = jnp.zeros_like(turned)
    lane_t = lax.broadcasted_iota(jnp.int32, columns.shape, 1)
    lane = lax.broadcasted_iota(jnp.int32, (8, size), 1)
    held[...] = jnp.zeros_like(held)
    cov[...] = cov_ref[...]
    panel[...] = cov_ref[0:NB, :]

    def column_step(t, row):
        shift = jnp.sum(jnp.where(lane_t == t, columns[...], 0.0), axis=1, keepdims=True)
        column = jnp.sum(plain[flags[t, 0]] * row, axis=1, keepdims=True) + shift
        turned[...] = jnp.where(lane_t == t, column, turned[...])
        return column

    def row_step(t, column):
        row = jnp.sum(plain_t[flags[t, 0]] * column, axis=0, keepdims=True) + shifts[pl.ds(t, 1), :]
        lines[pl.ds(t, 1), :] = row
        return row

    def block(b):
        start = pl.multiple_of(b * NB, NB)
        before = held[...]
        rows = panel[...]
        corner = pltpu.roll(rows, lax.rem(size - start, size), 1)[:, 0:128]
        wide = [jnp.broadcast_to(corner[:, k : k + 1], (NB, 128)) for k in range(NB)]
        d = [[None] * NB for _ in range(NB)]
        for k in range(NB):
            for i in range(k + 1):
                d[i][k] = jnp.broadcast_to(wide[k][i : i + 1, :], (8, 128))
        lines_b = [jnp.broadcast_to(panel[i : i + 1, :], (8, size)) for i in range(NB)]
        spread = lambda v: jnp.concatenate([v] * (size // 128), axis=1)
        for j in range(NB):
            pivot = d[j][j]
            r = lax.rsqrt(pivot)
            r = r * (1.5 - 0.5 * pivot * r * r)
            held[j : j + 1, :] = jnp.where(lane >= start + j, lines_b[j] * spread(r), 0.0)[0:1, :]
            if j == NB - 1:
                break
            inverse = 1.0 / pivot
            for i in range(j + 1, NB):
                ratio = d[j][i] * inverse
                for k in range(i, NB):
                    d[i][k] = d[i][k] - ratio * d[j][k]
                lines_b[i] = lines_b[i] - spread(ratio) * lines_b[j]
        cov[...] = cov[...] - gram3(before)
        done = held[...]
        out_ref[pl.ds(start, NB), :] = done
        after = lax.rem(start + NB, size)
        following = pltpu.roll(done, lax.rem(size - after, size), 1)[:, 0:128]
        h, m, l = split3(done)
        p, q, s = split3(following)
        lhs = jnp.concatenate([p, p, q, p, s, q], axis=0)
        rhs = jnp.concatenate([h, m, h, l, h, m], axis=0)
        change = lax.dot_general(lhs, rhs, TN_DIMS, preferred_element_type=F32)
        panel[...] = cov[pl.ds(pl.multiple_of(after, NB), NB), :] - change[0:NB, :]

    pairs = size // (2 * NB)
    turns = -(-steps // (2 * pairs))

    def two_blocks(v, row):
        for i in range(turns):
            t = 2 * (v * turns + i)
            row = row_step(t + 1, column_step(t, row))
        block(2 * v)
        block(2 * v + 1)
        return row

    lax.fori_loop(0, pairs, two_blocks, start_mean[...])
    lines[...] = lines[...] + turned[...].T
    for i in range(steps // per):

        @pl.when(tm == i)
        def _():
            mean_ref[...] = lines[i * per : (i + 1) * per, :]


def state(per, flags, cov, transition, update_map, init_mean, shifts, grads):
    size = transition.shape[0]
    steps = shifts.shape[0]
    padded = -(-steps // 128) * 128
    return pl.pallas_call(
        functools.partial(state_kernel, per),
        in_specs=[SMEM] + [VMEM] * 6,
        out_specs=[VMEM] * 3,
        out_shape=[
            jax.ShapeDtypeStruct((size, size), F32),
            jax.ShapeDtypeStruct((per, size), F32),
            jax.ShapeDtypeStruct(grads.shape, F32),
        ],
        scratch_shapes=[
            pltpu.VMEM((size, size), F32),
            pltpu.VMEM((NB, size), F32),
            pltpu.VMEM((NB, size), F32),
            pltpu.VMEM((2, size, size), F32),
            pltpu.VMEM((2, size, size), F32),
            pltpu.VMEM((padded, size), F32),
            pltpu.VMEM((size, padded), F32),
            pltpu.VMEM((padded, size), F32),
            pltpu.VMEM((size, padded), F32),
        ],
        compiler_params=pltpu.CompilerParams(vmem_limit_bytes=60 * 2**20),
    )(flags, cov, transition, update_map, init_mean[None], shifts, grads)


def local(frames, conv_taps, pooling, gain_matrix, transition, update_map, quiet_root, observed_root, init_mean, init_root, observed):
    shifts, flags, grads, cov = observe(
        observed, conv_taps.T, frames, pooling, gain_matrix.T, transition, update_map, quiet_root, observed_root, init_root
    )
    roots, filtered_means, grads = state(frames.shape[0], flags, cov, transition, update_map, init_mean, shifts, grads)
    return (filtered_means, roots[None], grads.T[None])


def solution(mesh):
    return jax.shard_map(
        local,
        mesh=mesh,
        in_specs=(
            P(("groups", "tm"), "chan", "space", None),
            P("chan", None),
            P("space", None),
            P(None, ("space", "chan")),
            P(),
            P(),
            P(),
            P(),
            P("groups"),
            P("groups", None),
            P(("groups", "tm")),
        ),
        out_specs=(
            P(("groups", "tm"), None),
            P(("groups", "tm"), None, None),
            P(("groups", "tm"), "chan", None),
        ),
        check_vma=False,
    )
```

```python
import functools

import jax
import jax.numpy as jnp
from jax import lax
from jax.experimental import pallas as pl
from jax.experimental.pallas import tpu as pltpu
from jax.sharding import PartitionSpec as P

DILATION_STEP = 2
NB = 16
F32 = jnp.float32
BF16 = jnp.bfloat16
VMEM = pl.BlockSpec(memory_space=pltpu.VMEM)
SMEM = pl.BlockSpec(memory_space=pltpu.SMEM)

NT_DIMS = (((1,), (1,)), ((), ()))
TN_DIMS = (((0,), (0,)), ((), ()))
PAIRS = (((0, 0), 0), ((1, 1), 1), ((-1, -1), 2), ((0, 1), 3), ((-1, 0), 3), ((-1, 1), 4))


MESH = pl.DeviceIdType.MESH


def fold_grads(grads, kind, gram, rows, group, owner, row_h, col_h, allowed, limit, wide):
    folded = jnp.zeros((rows, group * rows), F32)
    for c in range(group):
        folded = jnp.where(owner == c, gram[c * rows : (c + 1) * rows, :], folded)
    for a in range(-1, 2):
        for z in range(-1, 2):
            h = row_h - DILATION_STEP * a
            keep = (h >= 0) & (h < limit) & (row_h - col_h == DILATION_STEP * (a - z)) & allowed
            row = jnp.sum(jnp.where(keep, folded, 0.0), axis=0, keepdims=True)
            for (b, y), which in PAIRS:
                if which != kind:
                    continue
                k, q = 3 * (a + 1) + b + 1, 3 * (z + 1) + y + 1
                grads[k] = grads[k] + row * wide[q]
                if b != y:
                    grads[q] = grads[q] + row * wide[k]


def gram_grads(blocks, flags, wide, rows, group, row_h, col_h, allowed, limit):
    size, width = blocks[0].shape
    reach = DILATION_STEP
    lane = lax.broadcasted_iota(jnp.int32, (size, width), 1)
    left, low, high, one, two = [], [], [], [], []
    for t, block in enumerate(blocks):
        x = block.astype(F32)
        scaled = x * flags[t]
        left.append(scaled.astype(BF16))
        low.append(jnp.where(lane >= reach, scaled, 0.0).astype(BF16))
        high.append(jnp.where(lane < width - reach, scaled, 0.0).astype(BF16))
        one.append(jnp.where(lane < width - reach, pltpu.roll(x, width - reach, 1), 0.0).astype(BF16))
        two.append(jnp.where(lane < width - 2 * reach, pltpu.roll(x, width - 2 * reach, 1), 0.0).astype(BF16))
    cat = lambda pieces: jnp.concatenate(pieces, axis=1)
    left, plain = cat(left), cat(blocks)
    owner = lax.div(lax.broadcasted_iota(jnp.int32, (rows, size), 1), rows)
    grads = [jnp.zeros((1, size), F32) for _ in range(9)]
    for kind, (lhs, rhs) in enumerate(((left, plain), (cat(low), plain), (cat(high), plain), (left, cat(one)), (left, cat(two)))):
        gram = lax.dot_general(lhs, rhs, NT_DIMS, preferred_element_type=F32)
        fold_grads(grads, kind, gram, rows, group, owner, row_h, col_h, allowed, limit, wide)
    return grads


def observe_kernel(sizes, flags, taps, x_ref, pooling, gains, quiet_map, seen_map, quiet_root, seen_root, init_root,
                   shift_ref, flag_ref, grad_ref, cov,
                   tops, bottoms, lows, highs, pools, sums, grads_all, slots, grad_slots, flag_slots, maps, maps_t, grams,
                   halo_send, halo_recv, send_sem, recv_sem, grad_send, grad_recv, flag_send, flag_recv):
    n_tm, n_space, n_chan = sizes
    steps, channels, rows, width = x_ref.shape
    reach = DILATION_STEP
    group = min(channels, 256 // rows)
    groups = channels // group
    size = group * rows
    pack = group * reach
    n_all = n_tm * n_space * n_chan
    tm, space, chan = lax.axis_index("tm"), lax.axis_index("space"), lax.axis_index("chan")
    me = (tm * n_space + space) * n_chan + chan

    def place(p):
        return {"tm": lax.div(p, n_space * n_chan), "space": lax.rem(lax.div(p, n_chan), n_space), "chan": lax.rem(p, n_chan)}

    barrier = pltpu.get_barrier_semaphore()

    def greet(i, carry):
        pl.semaphore_signal(barrier, inc=1, device_id=place(lax.rem(me + i, n_all)), device_id_type=MESH)
        return carry

    lax.fori_loop(1, n_all, greet, 0)

    def pick(count, first_row):
        r = lax.broadcasted_iota(jnp.int32, (count, size), 0)
        c = lax.broadcasted_iota(jnp.int32, (count, size), 1)
        return jnp.where(c == lax.div(r, reach) * rows + lax.rem(r, reach) + first_row, 1.0, 0.0).astype(BF16)

    pick_top, pick_bottom = pick(pack, 0), pick(pack, rows - reach)
    for t in range(steps):
        for g in range(groups):
            x = x_ref[t, g * group : (g + 1) * group].reshape(size, width)
            at = pl.ds((g * steps + t) * pack, pack)
            tops[at, :] = jnp.dot(pick_top, x, preferred_element_type=F32).astype(BF16)
            bottoms[at, :] = jnp.dot(pick_bottom, x, preferred_element_type=F32).astype(BF16)
    prepare_chain(steps, quiet_map, seen_map, quiet_root, seen_root, init_root, maps, maps_t, grams, cov)
    for t in range(steps):
        flag_slots[tm, t : t + 1, :] = jnp.zeros((1, 128), F32) + flags[t].astype(F32)
    pl.semaphore_wait(barrier, n_all - 1)
    down = pltpu.make_async_remote_copy(
        src_ref=bottoms, dst_ref=lows, send_sem=halo_send.at[0], recv_sem=halo_recv.at[0],
        device_id={"space": lax.rem(space + 1, n_space)}, device_id_type=MESH)
    up = pltpu.make_async_remote_copy(
        src_ref=tops, dst_ref=highs, send_sem=halo_send.at[1], recv_sem=halo_recv.at[1],
        device_id={"space": lax.rem(space + n_space - 1, n_space)}, device_id_type=MESH)
    has_next, has_last = space < n_space - 1, space > 0

    @pl.when(has_next)
    def _():
        down.start()

    @pl.when(has_last)
    def _():
        up.start()

    def flag_copy(p, slot):
        return pltpu.make_async_remote_copy(
            src_ref=flag_slots.at[slot], dst_ref=flag_slots.at[slot], send_sem=flag_send.at[p], recv_sem=flag_recv.at[slot],
            device_id={"tm": p}, device_id_type=MESH)

    def each(count, mine, act):
        def turn(i, carry):
            act(lax.rem(mine + i, count))
            return carry

        lax.fori_loop(1, count, turn, 0)

    each(n_tm, tm, lambda p: flag_copy(p, tm).start())

    pool = pooling[...]
    row_i = lax.broadcasted_iota(jnp.int32, (rows, width), 0)
    lane_i = lax.broadcasted_iota(jnp.int32, (rows, width), 1)
    for b in range(-1, 2):
        moved = pool
        if b:
            moved = pltpu.roll(pool, (reach * b) % width, 1)
            moved = jnp.where((lane_i >= reach * b) & (lane_i < width + reach * b), moved, 0.0)
        for a in range(-1, 2):
            turned = moved
            if a:
                turned = pltpu.roll(moved, (reach * a) % rows, 0)
                turned = jnp.where((row_i >= reach * a) & (row_i < rows + reach * a), turned, 0.0)
            pools[3 * (a + 1) + b + 1] = turned
    flag_values = [flags[t].astype(F32) for t in range(steps)]

    def widened(first, count, each):
        owner = lax.div(lax.broadcasted_iota(jnp.int32, (1, count * each), 1), each)
        wide = []
        for k in range(9):
            row = jnp.zeros((1, count * each), F32)
            for c in range(count):
                row = jnp.where(owner == c, taps[k, first + c], row)
            wide.append(row)
        return wide

    def reduced(grads, first, count, each):
        stack = jnp.concatenate(grads + [jnp.zeros((7, count * each), F32)], axis=0)
        r = lax.broadcasted_iota(jnp.int32, (count * each, 128), 0)
        c = lax.broadcasted_iota(jnp.int32, (count * each, 128), 1)
        ones = jnp.where(c == first + lax.div(r, each), 1.0, 0.0).astype(BF16)
        h, m, l = split3(stack)
        dot = lambda part: jnp.dot(part, ones, preferred_element_type=F32)
        return dot(h) + (dot(m) + dot(l))

    grads_all[...] = jnp.zeros_like(grads_all)
    row_e = lax.broadcasted_iota(jnp.int32, (rows, size), 0)
    col_e = lax.rem(lax.broadcasted_iota(jnp.int32, (rows, size), 1), rows)

    def interior(g, carry):
        first = g * group
        for c in range(group):
            weight = taps[0, first + c] * pools[0]
            for k in range(1, 9):
                weight = weight + taps[k, first + c] * pools[k]
            for t in range(steps):
                part = x_ref[t, first + c].astype(F32) * weight
                sums[t, pl.ds(first + c, 1), :] = jnp.sum(part, axis=0, keepdims=True)
        blocks = [x_ref[t, pl.ds(first, group)].reshape(size, width) for t in range(steps)]
        grads = gram_grads(blocks, flag_values, widened(first, group, rows), rows, group, row_e, col_e, row_e >= 0, rows)
        grads_all[...] += reduced(grads, first, group, rows)
        return carry

    lax.fori_loop(0, groups, interior, 0)

    @pl.when(has_last)
    def _():
        up.wait_send()
        down.wait_recv()

    @pl.when(has_next)
    def _():
        down.wait_send()
        up.wait_recv()

    edge = 8 * reach
    half = group * edge
    r = lax.broadcasted_iota(jnp.int32, (half, size), 0)
    c = lax.broadcasted_iota(jnp.int32, (half, size), 1)
    e = lax.rem(r, edge)

    def position(e):
        return jnp.where(e < 4 * reach, e - reach, e + rows - 6 * reach)

    def real(e):
        return lax.rem(e, 4 * reach) < 3 * reach

    def halo(e):
        return (position(e) < 0) | (position(e) >= rows)

    own = jnp.where(real(e) & ~halo(e) & (c == lax.div(r, edge) * rows + position(e)), 1.0, 0.0).astype(BF16)
    r = lax.broadcasted_iota(jnp.int32, (half, pack), 0)
    c = lax.broadcasted_iota(jnp.int32, (half, pack), 1)
    e = lax.rem(r, edge)
    from_low = jnp.where((e < reach) & (c == lax.div(r, edge) * reach + e), 1.0, 0.0).astype(BF16)
    from_high = jnp.where((e >= 6 * reach) & (e < 7 * reach) & (c == lax.div(r, edge) * reach + e - 6 * reach), 1.0, 0.0).astype(BF16)
    edge_row = lax.broadcasted_iota(jnp.int32, (edge, width), 0)
    edge_pools = []
    for b in range(3):
        shifted = pools[3 + b]
        low_part = jnp.where(edge_row < reach, shifted[0:edge, :], 0.0)
        high_part = jnp.where((edge_row >= 6 * reach) & (edge_row < 7 * reach), pltpu.roll(shifted[rows - edge : rows, :], edge - reach, 0), 0.0)
        edge_pools.append((low_part, high_part))
    many = 2 * group
    e_row = lax.broadcasted_iota(jnp.int32, (edge, many * edge), 0)
    e_col = lax.rem(lax.broadcasted_iota(jnp.int32, (edge, many * edge), 1), edge)
    allowed = ((e_row < 4 * reach) == (e_col < 4 * reach)) & real(e_row) & real(e_col) & (halo(e_row) | halo(e_col))

    def outer(v, carry):
        blocks = []
        for t in range(steps):
            halves = []
            for q in range(2):
                g = 2 * v + q
                x = x_ref[t, pl.ds(g * group, group)].reshape(size, width)
                at = pl.ds(pl.multiple_of((g * steps + t) * pack, pack), pack)
                low_rows = jnp.where(has_last, lows[at, :].astype(F32), 0.0).astype(BF16)
                high_rows = jnp.where(has_next, highs[at, :].astype(F32), 0.0).astype(BF16)
                dot = lambda m, y: jnp.dot(m, y, preferred_element_type=F32)
                halves.append(dot(own, x) + dot(from_low, low_rows) + dot(from_high, high_rows))
            blocks.append(jnp.concatenate(halves, axis=0))
        first = v * many
        for i in range(many):
            weight = jnp.zeros((edge, width), F32)
            for b in range(3):
                low_part, high_part = edge_pools[b]
                weight = weight + taps[b, first + i] * low_part + taps[6 + b, first + i] * high_part
            for t in range(steps):
                part = blocks[t][i * edge : (i + 1) * edge, :] * weight
                at = pl.ds(first + i, 1)
                sums[t, at, :] = sums[t, at, :] + jnp.sum(part, axis=0, keepdims=True)
        grads = gram_grads([y.astype(BF16) for y in blocks], flag_values, widened(first, many, edge), edge, many, position(e_row), position(e_col), allowed, rows)
        grads_all[...] += reduced(grads, first, many, edge)
        return carry

    lax.fori_loop(0, groups // 2, outer, 0)

    scale = 1.0 / (rows * n_space * width)
    grad_slots[space] = grads_all[...] * scale
    for t in range(steps):
        tile = jnp.sum(sums[t], axis=1, keepdims=True)
        share = jnp.sum(tile * gains[...], axis=0, keepdims=True) * flag_values[t]
        slots[me, pl.ds(t, 1), :] = share

    def share_copy(p, slot):
        return pltpu.make_async_remote_copy(
            src_ref=slots.at[slot], dst_ref=slots.at[slot], send_sem=send_sem.at[p], recv_sem=recv_sem.at[slot],
            device_id=place(p), device_id_type=MESH)

    def grad_copy(s, slot):
        return pltpu.make_async_remote_copy(
            src_ref=grad_slots.at[slot], dst_ref=grad_slots.at[slot], send_sem=grad_send.at[s], recv_sem=grad_recv.at[slot],
            device_id={"space": s}, device_id_type=MESH)

    each(n_all, me, lambda p: share_copy(p, me).start())
    each(n_space, space, lambda s: grad_copy(s, space).start())
    each(n_tm, tm, lambda p: flag_copy(p, p).wait_recv())
    for block in range(n_tm):
        for t in range(steps):
            flag_ref[block * steps + t : block * steps + t + 1, :] = jnp.where(flag_slots[block, t : t + 1, :] > 0.5, 1, 0)
    run_chain(steps, tm, flag_ref, maps, maps_t, grams, cov)
    each(n_all, me, lambda p: share_copy(p, p).wait_recv())
    each(n_space, space, lambda s: grad_copy(s, s).wait_recv())
    for block in range(n_tm):
        total = slots[block * n_space * n_chan, 0:steps, :]
        for part in range(1, n_space * n_chan):
            total = total + slots[block * n_space * n_chan + part, 0:steps, :]
        shift_ref[block * steps : (block + 1) * steps, :] = total
    total = grad_slots[0]
    for part in range(1, n_space):
        total = total + grad_slots[part]
    grad_ref[...] = total[0:9, 0:channels]
    each(n_all, me, lambda p: share_copy(p, me).wait_send())
    each(n_space, space, lambda s: grad_copy(s, space).wait_send())
    each(n_tm, tm, lambda p: flag_copy(p, tm).wait_send())


def observe(flags, taps, frames, pooling, gains, transition, update_map, quiet_root, observed_root, init_root):
    steps, channels, rows, width = frames.shape
    states = gains.shape[1]
    sizes = tuple(lax.axis_size(name) for name in ("tm", "space", "chan"))
    n_all = sizes[0] * sizes[1] * sizes[2]
    packed = steps * channels * DILATION_STEP
    choices = 4 if steps % 2 == 0 else 2
    return pl.pallas_call(
        functools.partial(observe_kernel, sizes),
        in_specs=[SMEM, SMEM] + [VMEM] * 8,
        out_specs=[VMEM] * 4,
        out_shape=[
            jax.ShapeDtypeStruct((sizes[0] * steps, states), F32),
            jax.ShapeDtypeStruct((sizes[0] * steps, 128), jnp.int32),
            jax.ShapeDtypeStruct((9, channels), F32),
            jax.ShapeDtypeStruct((states, states), F32),
        ],
        scratch_shapes=[pltpu.VMEM((packed, width), BF16)] * 4 + [
            pltpu.VMEM((9, rows, width), F32),
            pltpu.VMEM((steps, channels, width), F32),
            pltpu.VMEM((16, 128), F32),
            pltpu.VMEM((n_all, 8 * (-(-steps // 8)), states), F32),
            pltpu.VMEM((sizes[1], 16, 128), F32),
            pltpu.VMEM((sizes[0], 8 * (-(-steps // 8)), 128), F32),
            pltpu.VMEM((choices, states, 3 * states), BF16),
            pltpu.VMEM((choices, 3 * states, states), BF16),
            pltpu.VMEM((choices, states, states), F32),
            pltpu.SemaphoreType.DMA((2,)),
            pltpu.SemaphoreType.DMA((2,)),
            pltpu.SemaphoreType.DMA((n_all,)),
            pltpu.SemaphoreType.DMA((n_all,)),
            pltpu.SemaphoreType.DMA((sizes[1],)),
            pltpu.SemaphoreType.DMA((sizes[1],)),
            pltpu.SemaphoreType.DMA((sizes[0],)),
            pltpu.SemaphoreType.DMA((sizes[0],)),
        ],
        compiler_params=pltpu.CompilerParams(collective_id=0, has_side_effects=True, vmem_limit_bytes=60 * 2**20),
    )(flags, taps, frames, pooling, gains, transition, update_map, quiet_root, observed_root, init_root)


def split2(x):
    high = x.astype(BF16)
    return high, (x - high.astype(F32)).astype(BF16)


def split3(x):
    high = x.astype(BF16)
    rest = x - high.astype(F32)
    mid = rest.astype(BF16)
    return high, mid, (rest - mid.astype(F32)).astype(BF16)


def gram3(x):
    h, m, l = split3(x)
    lhs = jnp.concatenate([h, h, m, h, l, m], axis=0)
    rhs = jnp.concatenate([h, m, h, l, h, m], axis=0)
    return lax.dot_general(lhs, rhs, TN_DIMS, preferred_element_type=F32)


def left_form(x):
    h, l = split2(x)
    return jnp.concatenate([h, h, l], axis=1)


def right_form(x):
    h, l = split2(x)
    return jnp.concatenate([h, l, h], axis=0)


def right_map(x):
    h, l = split2(x)
    return jnp.concatenate([h, h, l], axis=0)


def left_moving(x):
    h, l = split2(x)
    return jnp.concatenate([h, l, h], axis=1)


def product(lhs, rhs):
    return jnp.dot(lhs, rhs, preferred_element_type=F32)


def prepare_chain(steps, quiet_map, seen_map, quiet_root, seen_root, init_root, maps, maps_t, grams, cov):
    cov[...] = gram3(init_root[...])
    grams[0], grams[1] = gram3(quiet_root[...]), gram3(seen_root[...])
    single = [(quiet_map[...], grams[0]), (seen_map[...], grams[1])]
    if steps % 2:
        joined = single
    else:
        joined = []
        for index, (later, noise) in enumerate(single):
            lhs = left_form(later)
            maps_t[index] = right_map(later.T)
            rhs = maps_t[index]
            for earlier, earlier_noise in single:
                moved = product(lhs, right_form(earlier_noise))
                joined.append((product(lhs, right_form(earlier)), product(left_moving(moved), rhs) + noise))
    for index, (both, noise) in enumerate(joined):
        maps[index] = left_form(both)
        maps_t[index] = right_map(both.T)
        grams[index] = noise


def run_chain(steps, tm, flag_ref, maps, maps_t, grams, cov):
    paired = steps % 2 == 0

    def advance(t, carry):
        if paired:
            which = 2 * flag_ref[2 * t + 1, 0] + flag_ref[2 * t, 0]
        else:
            which = flag_ref[t, 0]
        moved = product(maps[which], right_form(cov[...]))
        cov[...] = product(left_moving(moved), maps_t[which]) + grams[which]
        return carry

    lax.fori_loop(0, (tm + 1) * (steps // 2 if paired else steps), advance, 0)


def state_kernel(per, flags, cov_ref, quiet_map, seen_map, start_mean, shift_ref, grad_in, out_ref, mean_ref, grad_ref,
                 cov, panel, held, plain, plain_t, shifts, columns, lines, turned):
    size = out_ref.shape[0]
    steps = shift_ref.shape[0]
    tm = lax.axis_index("tm")
    for k in range(grad_in.shape[0]):
        grad_ref[k] = grad_in[k : k + 1, :]
    for index, map_ref in enumerate((quiet_map, seen_map)):
        plain[index] = map_ref[...]
        plain_t[index] = map_ref[...].T
    shifts[...] = jnp.zeros_like(shifts)
    shifts[0:steps, :] = shift_ref[...]
    columns[...] = shifts[...].T
    lines[...] = jnp.zeros_like(lines)
    turned[...] = jnp.zeros_like(turned)
    lane_t = lax.broadcasted_iota(jnp.int32, columns.shape, 1)
    lane = lax.broadcasted_iota(jnp.int32, (NB, size), 1)
    line = lax.broadcasted_iota(jnp.int32, (NB, size), 0)
    held[...] = jnp.zeros_like(held)
    cov[...] = cov_ref[...]
    panel[...] = cov_ref[0:NB, :]

    def column_step(t, row):
        shift = jnp.sum(jnp.where(lane_t == t, columns[...], 0.0), axis=1, keepdims=True)
        column = jnp.sum(plain[flags[t, 0]] * row, axis=1, keepdims=True) + shift
        turned[...] = jnp.where(lane_t == t, column, turned[...])
        return column

    def row_step(t, column):
        row = jnp.sum(plain_t[flags[t, 0]] * column, axis=0, keepdims=True) + shifts[pl.ds(t, 1), :]
        lines[pl.ds(t, 1), :] = row
        return row

    def block(b):
        start = pl.multiple_of(b * NB, NB)
        before = held[...]
        rows = panel[...]
        corner = pltpu.roll(rows, lax.rem(size - start, size), 1)[:, 0:128]
        wide = [jnp.broadcast_to(corner[:, k : k + 1], (NB, 128)) for k in range(NB)]
        row_n = lax.broadcasted_iota(jnp.int32, (NB, 128), 0)
        spread = lambda v: jnp.concatenate([v] * (size // 128), axis=1)
        scales = jnp.zeros((NB, 128), F32)
        for j in range(NB):
            pivot = jnp.broadcast_to(wide[j][j : j + 1, :], (NB, 128))
            scales = jnp.where(row_n == j, pivot, scales)
            if j == NB - 1:
                break
            inverse = pl.reciprocal(pivot, approx=True)
            inverse = inverse * (2.0 - pivot * inverse)
            ratio = jnp.where(row_n > j, wide[j] * inverse, 0.0)
            for k in range(j + 1, NB):
                wide[k] = wide[k] - ratio * jnp.broadcast_to(wide[k][j : j + 1, :], (NB, 128))
            rows = rows - spread(ratio) * jnp.broadcast_to(rows[j : j + 1, :], (NB, size))
        r = lax.rsqrt(scales)
        r = r * (1.5 - 0.5 * scales * r * r)
        held[...] = jnp.where(lane >= start + line, rows * spread(r), 0.0)
        cov[...] = cov[...] - gram3(before)
        done = held[...]
        out_ref[pl.ds(start, NB), :] = done
        after = lax.rem(start + NB, size)
        following = pltpu.roll(done, lax.rem(size - after, size), 1)[:, 0:128]
        h, m, l = split3(done)
        p, q, s = split3(following)
        lhs = jnp.concatenate([p, p, q, p, s, q], axis=0)
        rhs = jnp.concatenate([h, m, h, l, h, m], axis=0)
        change = lax.dot_general(lhs, rhs, TN_DIMS, preferred_element_type=F32)
        panel[...] = cov[pl.ds(pl.multiple_of(after, NB), NB), :] - change[0:NB, :]

    pairs = size // (2 * NB)
    turns = -(-steps // (2 * pairs))

    def two_blocks(v, row):
        for i in range(turns):
            t = 2 * (v * turns + i)
            row = row_step(t + 1, column_step(t, row))
        block(2 * v)
        block(2 * v + 1)
        return row

    lax.fori_loop(0, pairs, two_blocks, start_mean[...])
    lines[...] = lines[...] + turned[...].T
    for i in range(steps // per):

        @pl.when(tm == i)
        def _():
            mean_ref[...] = lines[i * per : (i + 1) * per, :]


def state(per, flags, cov, transition, update_map, init_mean, shifts, grads):
    size = transition.shape[0]
    steps = shifts.shape[0]
    padded = -(-steps // 128) * 128
    return pl.pallas_call(
        functools.partial(state_kernel, per),
        in_specs=[SMEM] + [VMEM] * 6,
        out_specs=[VMEM] * 3,
        out_shape=[
            jax.ShapeDtypeStruct((size, size), F32),
            jax.ShapeDtypeStruct((per, size), F32),
            jax.ShapeDtypeStruct((grads.shape[0], 1, grads.shape[1]), F32),
        ],
        scratch_shapes=[
            pltpu.VMEM((size, size), F32),
            pltpu.VMEM((NB, size), F32),
            pltpu.VMEM((NB, size), F32),
            pltpu.VMEM((2, size, size), F32),
            pltpu.VMEM((2, size, size), F32),
            pltpu.VMEM((padded, size), F32),
            pltpu.VMEM((size, padded), F32),
            pltpu.VMEM((padded, size), F32),
            pltpu.VMEM((size, padded), F32),
        ],
        compiler_params=pltpu.CompilerParams(vmem_limit_bytes=60 * 2**20),
    )(flags, cov, transition, update_map, init_mean[None], shifts, grads)


def local(frames, conv_taps, pooling, gain_matrix, transition, update_map, quiet_root, observed_root, init_mean, init_root, observed):
    shifts, flags, grads, cov = observe(
        observed, conv_taps.T, frames, pooling, gain_matrix.T, transition, update_map, quiet_root, observed_root, init_root
    )
    roots, filtered_means, grads = state(frames.shape[0], flags, cov, transition, update_map, init_mean, shifts, grads)
    return (filtered_means, roots[None], jnp.transpose(grads, (1, 2, 0)))


def solution(mesh):
    return jax.shard_map(
        local,
        mesh=mesh,
        in_specs=(
            P(("groups", "tm"), "chan", "space", None),
            P("chan", None),
            P("space", None),
            P(None, ("space", "chan")),
            P(),
            P(),
            P(),
            P(),
            P("groups"),
            P("groups", None),
            P(("groups", "tm")),
        ),
        out_specs=(
            P(("groups", "tm"), None),
            P(("groups", "tm"), None, None),
            P(("groups", "tm"), "chan", None),
        ),
        check_vma=False,
    )
```

```python
import functools

import jax
import jax.numpy as jnp
from jax import lax
from jax.experimental import pallas as pl
from jax.experimental.pallas import tpu as pltpu
from jax.sharding import PartitionSpec as P

DILATION_STEP = 2
NB = 16
F32 = jnp.float32
BF16 = jnp.bfloat16
VMEM = pl.BlockSpec(memory_space=pltpu.VMEM)
SMEM = pl.BlockSpec(memory_space=pltpu.SMEM)

NT_DIMS = (((1,), (1,)), ((), ()))
TN_DIMS = (((0,), (0,)), ((), ()))
PAIRS = (((0, 0), 0), ((1, 1), 1), ((-1, -1), 2), ((0, 1), 3), ((-1, 0), 3), ((-1, 1), 4))


MESH = pl.DeviceIdType.MESH


def fold_grads(grads, kind, gram, rows, group, owner, row_h, col_h, allowed, limit, wide):
    folded = jnp.zeros((rows, group * rows), F32)
    for c in range(group):
        folded = jnp.where(owner == c, gram[c * rows : (c + 1) * rows, :], folded)
    for a in range(-1, 2):
        for z in range(-1, 2):
            h = row_h - DILATION_STEP * a
            keep = (h >= 0) & (h < limit) & (row_h - col_h == DILATION_STEP * (a - z)) & allowed
            row = jnp.sum(jnp.where(keep, folded, 0.0), axis=0, keepdims=True)
            for (b, y), which in PAIRS:
                if which != kind:
                    continue
                k, q = 3 * (a + 1) + b + 1, 3 * (z + 1) + y + 1
                grads[k] = grads[k] + row * wide[q]
                if b != y:
                    grads[q] = grads[q] + row * wide[k]


def gram_grads(blocks, flags, wide, rows, group, row_h, col_h, allowed, limit):
    size, width = blocks[0].shape
    reach = DILATION_STEP
    lane = lax.broadcasted_iota(jnp.int32, (size, width), 1)
    left, low, high, one, two = [], [], [], [], []
    for t, block in enumerate(blocks):
        x = block.astype(F32)
        scaled = x * flags[t]
        left.append(scaled.astype(BF16))
        low.append(jnp.where(lane >= reach, scaled, 0.0).astype(BF16))
        high.append(jnp.where(lane < width - reach, scaled, 0.0).astype(BF16))
        one.append(jnp.where(lane < width - reach, pltpu.roll(x, width - reach, 1), 0.0).astype(BF16))
        two.append(jnp.where(lane < width - 2 * reach, pltpu.roll(x, width - 2 * reach, 1), 0.0).astype(BF16))
    cat = lambda pieces: jnp.concatenate(pieces, axis=1)
    left, plain = cat(left), cat(blocks)
    owner = lax.div(lax.broadcasted_iota(jnp.int32, (rows, size), 1), rows)
    grads = [jnp.zeros((1, size), F32) for _ in range(9)]
    for kind, (lhs, rhs) in enumerate(((left, plain), (cat(low), plain), (cat(high), plain), (left, cat(one)), (left, cat(two)))):
        gram = lax.dot_general(lhs, rhs, NT_DIMS, preferred_element_type=F32)
        fold_grads(grads, kind, gram, rows, group, owner, row_h, col_h, allowed, limit, wide)
    return grads


def observe_kernel(sizes, flags, taps, x_ref, pooling, gains, quiet_map, seen_map, quiet_root, seen_root, init_root,
                   shift_ref, flag_ref, grad_ref, cov,
                   tops, bottoms, lows, highs, pools, sums, grads_all, slots, grad_slots, flag_slots, maps, maps_t, grams,
                   halo_send, halo_recv, send_sem, recv_sem, grad_send, grad_recv, flag_send, flag_recv):
    n_tm, n_space, n_chan = sizes
    steps, channels, rows, width = x_ref.shape
    reach = DILATION_STEP
    group = min(channels, 256 // rows)
    groups = channels // group
    size = group * rows
    pack = group * reach
    n_all = n_tm * n_space * n_chan
    tm, space, chan = lax.axis_index("tm"), lax.axis_index("space"), lax.axis_index("chan")
    me = (tm * n_space + space) * n_chan + chan

    def place(p):
        return {"tm": lax.div(p, n_space * n_chan), "space": lax.rem(lax.div(p, n_chan), n_space), "chan": lax.rem(p, n_chan)}

    barrier = pltpu.get_barrier_semaphore()

    def greet(i, carry):
        pl.semaphore_signal(barrier, inc=1, device_id=place(lax.rem(me + i, n_all)), device_id_type=MESH)
        return carry

    lax.fori_loop(1, n_all, greet, 0)

    def pick(count, first_row):
        r = lax.broadcasted_iota(jnp.int32, (count, size), 0)
        c = lax.broadcasted_iota(jnp.int32, (count, size), 1)
        return jnp.where(c == lax.div(r, reach) * rows + lax.rem(r, reach) + first_row, 1.0, 0.0).astype(BF16)

    pick_top, pick_bottom = pick(pack, 0), pick(pack, rows - reach)
    for t in range(steps):
        for g in range(groups):
            x = x_ref[t, g * group : (g + 1) * group].reshape(size, width)
            at = pl.ds((g * steps + t) * pack, pack)
            tops[at, :] = jnp.dot(pick_top, x, preferred_element_type=F32).astype(BF16)
            bottoms[at, :] = jnp.dot(pick_bottom, x, preferred_element_type=F32).astype(BF16)
    pool = pooling[...]
    row_i = lax.broadcasted_iota(jnp.int32, (rows, width), 0)
    lane_i = lax.broadcasted_iota(jnp.int32, (rows, width), 1)
    for b in range(-1, 2):
        moved = pool
        if b:
            moved = pltpu.roll(pool, (reach * b) % width, 1)
            moved = jnp.where((lane_i >= reach * b) & (lane_i < width + reach * b), moved, 0.0)
        for a in range(-1, 2):
            turned = moved
            if a:
                turned = pltpu.roll(moved, (reach * a) % rows, 0)
                turned = jnp.where((row_i >= reach * a) & (row_i < rows + reach * a), turned, 0.0)
            pools[3 * (a + 1) + b + 1] = turned
    flag_values = [flags[t].astype(F32) for t in range(steps)]

    def widened(first, count, each):
        owner = lax.div(lax.broadcasted_iota(jnp.int32, (1, count * each), 1), each)
        wide = []
        for k in range(9):
            row = jnp.zeros((1, count * each), F32)
            for c in range(count):
                row = jnp.where(owner == c, taps[k, first + c], row)
            wide.append(row)
        return wide

    def reduced(grads, first, count, each):
        stack = jnp.concatenate(grads + [jnp.zeros((7, count * each), F32)], axis=0)
        r = lax.broadcasted_iota(jnp.int32, (count * each, 128), 0)
        c = lax.broadcasted_iota(jnp.int32, (count * each, 128), 1)
        ones = jnp.where(c == first + lax.div(r, each), 1.0, 0.0).astype(BF16)
        h, m, l = split3(stack)
        dot = lambda part: jnp.dot(part, ones, preferred_element_type=F32)
        return dot(h) + (dot(m) + dot(l))

    grads_all[...] = jnp.zeros_like(grads_all)
    row_e = lax.broadcasted_iota(jnp.int32, (rows, size), 0)
    col_e = lax.rem(lax.broadcasted_iota(jnp.int32, (rows, size), 1), rows)

    def interior(g, carry):
        first = g * group
        for c in range(group):
            weight = taps[0, first + c] * pools[0]
            for k in range(1, 9):
                weight = weight + taps[k, first + c] * pools[k]
            for t in range(steps):
                part = x_ref[t, first + c].astype(F32) * weight
                sums[t, pl.ds(first + c, 1), :] = jnp.sum(part, axis=0, keepdims=True)
        blocks = [x_ref[t, pl.ds(first, group)].reshape(size, width) for t in range(steps)]
        grads = gram_grads(blocks, flag_values, widened(first, group, rows), rows, group, row_e, col_e, row_e >= 0, rows)
        grads_all[...] += reduced(grads, first, group, rows)
        return carry

    lax.fori_loop(0, groups, interior, 0)

    for t in range(steps):
        flag_slots[tm, t : t + 1, :] = jnp.zeros((1, 128), F32) + flags[t].astype(F32)
    pl.semaphore_wait(barrier, n_all - 1)
    down = pltpu.make_async_remote_copy(
        src_ref=bottoms, dst_ref=lows, send_sem=halo_send.at[0], recv_sem=halo_recv.at[0],
        device_id={"space": lax.rem(space + 1, n_space)}, device_id_type=MESH)
    up = pltpu.make_async_remote_copy(
        src_ref=tops, dst_ref=highs, send_sem=halo_send.at[1], recv_sem=halo_recv.at[1],
        device_id={"space": lax.rem(space + n_space - 1, n_space)}, device_id_type=MESH)
    has_next, has_last = space < n_space - 1, space > 0

    @pl.when(has_next)
    def _():
        down.start()

    @pl.when(has_last)
    def _():
        up.start()

    def flag_copy(p, slot):
        return pltpu.make_async_remote_copy(
            src_ref=flag_slots.at[slot], dst_ref=flag_slots.at[slot], send_sem=flag_send.at[p], recv_sem=flag_recv.at[slot],
            device_id={"tm": p}, device_id_type=MESH)

    def each(count, mine, act):
        def turn(i, carry):
            act(lax.rem(mine + i, count))
            return carry

        lax.fori_loop(1, count, turn, 0)

    each(n_tm, tm, lambda p: flag_copy(p, tm).start())
    prepare_chain(steps, quiet_map, seen_map, quiet_root, seen_root, init_root, maps, maps_t, grams, cov)

    @pl.when(has_last)
    def _():
        up.wait_send()
        down.wait_recv()

    @pl.when(has_next)
    def _():
        down.wait_send()
        up.wait_recv()

    edge = 8 * reach
    half = group * edge
    r = lax.broadcasted_iota(jnp.int32, (half, size), 0)
    c = lax.broadcasted_iota(jnp.int32, (half, size), 1)
    e = lax.rem(r, edge)

    def position(e):
        return jnp.where(e < 4 * reach, e - reach, e + rows - 6 * reach)

    def real(e):
        return lax.rem(e, 4 * reach) < 3 * reach

    def halo(e):
        return (position(e) < 0) | (position(e) >= rows)

    own = jnp.where(real(e) & ~halo(e) & (c == lax.div(r, edge) * rows + position(e)), 1.0, 0.0).astype(BF16)
    r = lax.broadcasted_iota(jnp.int32, (half, pack), 0)
    c = lax.broadcasted_iota(jnp.int32, (half, pack), 1)
    e = lax.rem(r, edge)
    from_low = jnp.where((e < reach) & (c == lax.div(r, edge) * reach + e), 1.0, 0.0).astype(BF16)
    from_high = jnp.where((e >= 6 * reach) & (e < 7 * reach) & (c == lax.div(r, edge) * reach + e - 6 * reach), 1.0, 0.0).astype(BF16)
    edge_row = lax.broadcasted_iota(jnp.int32, (edge, width), 0)
    edge_pools = []
    for b in range(3):
        shifted = pools[3 + b]
        low_part = jnp.where(edge_row < reach, shifted[0:edge, :], 0.0)
        high_part = jnp.where((edge_row >= 6 * reach) & (edge_row < 7 * reach), pltpu.roll(shifted[rows - edge : rows, :], edge - reach, 0), 0.0)
        edge_pools.append((low_part, high_part))
    many = 2 * group
    e_row = lax.broadcasted_iota(jnp.int32, (edge, many * edge), 0)
    e_col = lax.rem(lax.broadcasted_iota(jnp.int32, (edge, many * edge), 1), edge)
    allowed = ((e_row < 4 * reach) == (e_col < 4 * reach)) & real(e_row) & real(e_col) & (halo(e_row) | halo(e_col))

    def outer(v, carry):
        blocks = []
        for t in range(steps):
            halves = []
            for q in range(2):
                g = 2 * v + q
                x = x_ref[t, pl.ds(g * group, group)].reshape(size, width)
                at = pl.ds(pl.multiple_of((g * steps + t) * pack, pack), pack)
                low_rows = jnp.where(has_last, lows[at, :].astype(F32), 0.0).astype(BF16)
                high_rows = jnp.where(has_next, highs[at, :].astype(F32), 0.0).astype(BF16)
                dot = lambda m, y: jnp.dot(m, y, preferred_element_type=F32)
                halves.append(dot(own, x) + dot(from_low, low_rows) + dot(from_high, high_rows))
            blocks.append(jnp.concatenate(halves, axis=0))
        first = v * many
        for i in range(many):
            weight = jnp.zeros((edge, width), F32)
            for b in range(3):
                low_part, high_part = edge_pools[b]
                weight = weight + taps[b, first + i] * low_part + taps[6 + b, first + i] * high_part
            for t in range(steps):
                part = blocks[t][i * edge : (i + 1) * edge, :] * weight
                at = pl.ds(first + i, 1)
                sums[t, at, :] = sums[t, at, :] + jnp.sum(part, axis=0, keepdims=True)
        grads = gram_grads([y.astype(BF16) for y in blocks], flag_values, widened(first, many, edge), edge, many, position(e_row), position(e_col), allowed, rows)
        grads_all[...] += reduced(grads, first, many, edge)
        return carry

    lax.fori_loop(0, groups // 2, outer, 0)

    scale = 1.0 / (rows * n_space * width)
    grad_slots[space] = grads_all[...] * scale
    for t in range(steps):
        tile = jnp.sum(sums[t], axis=1, keepdims=True)
        share = jnp.sum(tile * gains[...], axis=0, keepdims=True) * flag_values[t]
        slots[me, pl.ds(t, 1), :] = share

    def share_copy(p, slot):
        return pltpu.make_async_remote_copy(
            src_ref=slots.at[slot], dst_ref=slots.at[slot], send_sem=send_sem.at[p], recv_sem=recv_sem.at[slot],
            device_id=place(p), device_id_type=MESH)

    def grad_copy(s, slot):
        return pltpu.make_async_remote_copy(
            src_ref=grad_slots.at[slot], dst_ref=grad_slots.at[slot], send_sem=grad_send.at[s], recv_sem=grad_recv.at[slot],
            device_id={"space": s}, device_id_type=MESH)

    each(n_all, me, lambda p: share_copy(p, me).start())
    each(n_space, space, lambda s: grad_copy(s, space).start())
    each(n_tm, tm, lambda p: flag_copy(p, p).wait_recv())
    for block in range(n_tm):
        for t in range(steps):
            flag_ref[block * steps + t : block * steps + t + 1, :] = jnp.where(flag_slots[block, t : t + 1, :] > 0.5, 1, 0)
    run_chain(steps, tm, flag_ref, maps, maps_t, grams, cov)
    each(n_all, me, lambda p: share_copy(p, p).wait_recv())
    each(n_space, space, lambda s: grad_copy(s, s).wait_recv())
    for block in range(n_tm):
        total = slots[block * n_space * n_chan, 0:steps, :]
        for part in range(1, n_space * n_chan):
            total = total + slots[block * n_space * n_chan + part, 0:steps, :]
        shift_ref[block * steps : (block + 1) * steps, :] = total
    total = grad_slots[0]
    for part in range(1, n_space):
        total = total + grad_slots[part]
    grad_ref[...] = total[0:9, 0:channels]
    each(n_all, me, lambda p: share_copy(p, me).wait_send())
    each(n_space, space, lambda s: grad_copy(s, space).wait_send())
    each(n_tm, tm, lambda p: flag_copy(p, tm).wait_send())


def observe(flags, taps, frames, pooling, gains, transition, update_map, quiet_root, observed_root, init_root):
    steps, channels, rows, width = frames.shape
    states = gains.shape[1]
    sizes = tuple(lax.axis_size(name) for name in ("tm", "space", "chan"))
    n_all = sizes[0] * sizes[1] * sizes[2]
    packed = steps * channels * DILATION_STEP
    choices = 4 if steps % 2 == 0 else 2
    return pl.pallas_call(
        functools.partial(observe_kernel, sizes),
        in_specs=[SMEM, SMEM] + [VMEM] * 8,
        out_specs=[VMEM] * 4,
        out_shape=[
            jax.ShapeDtypeStruct((sizes[0] * steps, states), F32),
            jax.ShapeDtypeStruct((sizes[0] * steps, 128), jnp.int32),
            jax.ShapeDtypeStruct((9, channels), F32),
            jax.ShapeDtypeStruct((states, states), F32),
        ],
        scratch_shapes=[pltpu.VMEM((packed, width), BF16)] * 4 + [
            pltpu.VMEM((9, rows, width), F32),
            pltpu.VMEM((steps, channels, width), F32),
            pltpu.VMEM((16, 128), F32),
            pltpu.VMEM((n_all, 8 * (-(-steps // 8)), states), F32),
            pltpu.VMEM((sizes[1], 16, 128), F32),
            pltpu.VMEM((sizes[0], 8 * (-(-steps // 8)), 128), F32),
            pltpu.VMEM((choices, states, 3 * states), BF16),
            pltpu.VMEM((choices, 3 * states, states), BF16),
            pltpu.VMEM((choices, states, states), F32),
            pltpu.SemaphoreType.DMA((2,)),
            pltpu.SemaphoreType.DMA((2,)),
            pltpu.SemaphoreType.DMA((n_all,)),
            pltpu.SemaphoreType.DMA((n_all,)),
            pltpu.SemaphoreType.DMA((sizes[1],)),
            pltpu.SemaphoreType.DMA((sizes[1],)),
            pltpu.SemaphoreType.DMA((sizes[0],)),
            pltpu.SemaphoreType.DMA((sizes[0],)),
        ],
        compiler_params=pltpu.CompilerParams(collective_id=0, has_side_effects=True, vmem_limit_bytes=60 * 2**20),
    )(flags, taps, frames, pooling, gains, transition, update_map, quiet_root, observed_root, init_root)


def split2(x):
    high = x.astype(BF16)
    return high, (x - high.astype(F32)).astype(BF16)


def split3(x):
    high = x.astype(BF16)
    rest = x - high.astype(F32)
    mid = rest.astype(BF16)
    return high, mid, (rest - mid.astype(F32)).astype(BF16)


def gram3(x):
    h, m, l = split3(x)
    lhs = jnp.concatenate([h, h, m, h, l, m], axis=0)
    rhs = jnp.concatenate([h, m, h, l, h, m], axis=0)
    return lax.dot_general(lhs, rhs, TN_DIMS, preferred_element_type=F32)


def left_form(x):
    h, l = split2(x)
    return jnp.concatenate([h, h, l], axis=1)


def right_form(x):
    h, l = split2(x)
    return jnp.concatenate([h, l, h], axis=0)


def right_map(x):
    h, l = split2(x)
    return jnp.concatenate([h, h, l], axis=0)


def left_moving(x):
    h, l = split2(x)
    return jnp.concatenate([h, l, h], axis=1)


def product(lhs, rhs):
    return jnp.dot(lhs, rhs, preferred_element_type=F32)


def prepare_chain(steps, quiet_map, seen_map, quiet_root, seen_root, init_root, maps, maps_t, grams, cov):
    cov[...] = gram3(init_root[...])
    grams[0], grams[1] = gram3(quiet_root[...]), gram3(seen_root[...])
    single = [(quiet_map[...], grams[0]), (seen_map[...], grams[1])]
    if steps % 2:
        joined = single
    else:
        joined = []
        for index, (later, noise) in enumerate(single):
            lhs = left_form(later)
            maps_t[index] = right_map(later.T)
            rhs = maps_t[index]
            for earlier, earlier_noise in single:
                moved = product(lhs, right_form(earlier_noise))
                joined.append((product(lhs, right_form(earlier)), product(left_moving(moved), rhs) + noise))
    for index, (both, noise) in enumerate(joined):
        maps[index] = left_form(both)
        maps_t[index] = right_map(both.T)
        grams[index] = noise


def run_chain(steps, tm, flag_ref, maps, maps_t, grams, cov):
    paired = steps % 2 == 0

    def advance(t, carry):
        if paired:
            which = 2 * flag_ref[2 * t + 1, 0] + flag_ref[2 * t, 0]
        else:
            which = flag_ref[t, 0]
        moved = product(maps[which], right_form(cov[...]))
        cov[...] = product(left_moving(moved), maps_t[which]) + grams[which]
        return carry

    lax.fori_loop(0, (tm + 1) * (steps // 2 if paired else steps), advance, 0)


def state_kernel(per, flags, cov_ref, quiet_map, seen_map, start_mean, shift_ref, grad_in, out_ref, mean_ref, grad_ref,
                 cov, panel, held, plain, plain_t, shifts, columns, lines, turned):
    size = out_ref.shape[0]
    steps = shift_ref.shape[0]
    tm = lax.axis_index("tm")
    for k in range(grad_in.shape[0]):
        grad_ref[k] = grad_in[k : k + 1, :]
    for index, map_ref in enumerate((quiet_map, seen_map)):
        plain[index] = map_ref[...]
        plain_t[index] = map_ref[...].T
    shifts[...] = jnp.zeros_like(shifts)
    shifts[0:steps, :] = shift_ref[...]
    columns[...] = shifts[...].T
    lines[...] = jnp.zeros_like(lines)
    turned[...] = jnp.zeros_like(turned)
    lane_t = lax.broadcasted_iota(jnp.int32, columns.shape, 1)
    lane = lax.broadcasted_iota(jnp.int32, (NB, size), 1)
    line = lax.broadcasted_iota(jnp.int32, (NB, size), 0)
    held[...] = jnp.zeros_like(held)
    cov[...] = cov_ref[...]
    panel[...] = cov_ref[0:NB, :]

    def column_step(t, row):
        shift = jnp.sum(jnp.where(lane_t == t, columns[...], 0.0), axis=1, keepdims=True)
        column = jnp.sum(plain[flags[t, 0]] * row, axis=1, keepdims=True) + shift
        turned[...] = jnp.where(lane_t == t, column, turned[...])
        return column

    def row_step(t, column):
        row = jnp.sum(plain_t[flags[t, 0]] * column, axis=0, keepdims=True) + shifts[pl.ds(t, 1), :]
        lines[pl.ds(t, 1), :] = row
        return row

    def block(b):
        start = pl.multiple_of(b * NB, NB)
        before = held[...]
        rows = panel[...]
        corner = pltpu.roll(rows, lax.rem(size - start, size), 1)[:, 0:128]
        wide = [jnp.broadcast_to(corner[:, k : k + 1], (NB, 128)) for k in range(NB)]
        row_n = lax.broadcasted_iota(jnp.int32, (NB, 128), 0)
        spread = lambda v: jnp.concatenate([v] * (size // 128), axis=1)
        scales = jnp.zeros((NB, 128), F32)
        for j in range(NB):
            pivot = jnp.broadcast_to(wide[j][j : j + 1, :], (NB, 128))
            scales = jnp.where(row_n == j, pivot, scales)
            if j == NB - 1:
                break
            inverse = pl.reciprocal(pivot, approx=True)
            inverse = inverse * (2.0 - pivot * inverse)
            ratio = jnp.where(row_n > j, wide[j] * inverse, 0.0)
            for k in range(j + 1, NB):
                wide[k] = wide[k] - ratio * jnp.broadcast_to(wide[k][j : j + 1, :], (NB, 128))
            rows = rows - spread(ratio) * jnp.broadcast_to(rows[j : j + 1, :], (NB, size))
        r = lax.rsqrt(scales)
        r = r * (1.5 - 0.5 * scales * r * r)
        held[...] = jnp.where(lane >= start + line, rows * spread(r), 0.0)
        cov[...] = cov[...] - gram3(before)
        done = held[...]
        out_ref[pl.ds(start, NB), :] = done
        after = lax.rem(start + NB, size)
        following = pltpu.roll(done, lax.rem(size - after, size), 1)[:, 0:128]
        h, m, l = split3(done)
        p, q, s = split3(following)
        lhs = jnp.concatenate([p, p, q, p, s, q], axis=0)
        rhs = jnp.concatenate([h, m, h, l, h, m], axis=0)
        change = lax.dot_general(lhs, rhs, TN_DIMS, preferred_element_type=F32)
        panel[...] = cov[pl.ds(pl.multiple_of(after, NB), NB), :] - change[0:NB, :]

    pairs = size // (2 * NB)
    turns = -(-steps // (2 * pairs))

    def two_blocks(v, row):
        for i in range(turns):
            t = 2 * (v * turns + i)
            row = row_step(t + 1, column_step(t, row))
        block(2 * v)
        block(2 * v + 1)
        return row

    lax.fori_loop(0, pairs, two_blocks, start_mean[...])
    lines[...] = lines[...] + turned[...].T
    for i in range(steps // per):

        @pl.when(tm == i)
        def _():
            mean_ref[...] = lines[i * per : (i + 1) * per, :]


def state(per, flags, cov, transition, update_map, init_mean, shifts, grads):
    size = transition.shape[0]
    steps = shifts.shape[0]
    padded = -(-steps // 128) * 128
    return pl.pallas_call(
        functools.partial(state_kernel, per),
        in_specs=[SMEM] + [VMEM] * 6,
        out_specs=[VMEM] * 3,
        out_shape=[
            jax.ShapeDtypeStruct((size, size), F32),
            jax.ShapeDtypeStruct((per, size), F32),
            jax.ShapeDtypeStruct((grads.shape[0], 1, grads.shape[1]), F32),
        ],
        scratch_shapes=[
            pltpu.VMEM((size, size), F32),
            pltpu.VMEM((NB, size), F32),
            pltpu.VMEM((NB, size), F32),
            pltpu.VMEM((2, size, size), F32),
            pltpu.VMEM((2, size, size), F32),
            pltpu.VMEM((padded, size), F32),
            pltpu.VMEM((size, padded), F32),
            pltpu.VMEM((padded, size), F32),
            pltpu.VMEM((size, padded), F32),
        ],
        compiler_params=pltpu.CompilerParams(vmem_limit_bytes=60 * 2**20),
    )(flags, cov, transition, update_map, init_mean[None], shifts, grads)


def local(frames, conv_taps, pooling, gain_matrix, transition, update_map, quiet_root, observed_root, init_mean, init_root, observed):
    shifts, flags, grads, cov = observe(
        observed, conv_taps.T, frames, pooling, gain_matrix.T, transition, update_map, quiet_root, observed_root, init_root
    )
    roots, filtered_means, grads = state(frames.shape[0], flags, cov, transition, update_map, init_mean, shifts, grads)
    return (filtered_means, roots[None], jnp.transpose(grads, (1, 2, 0)))


def solution(mesh):
    return jax.shard_map(
        local,
        mesh=mesh,
        in_specs=(
            P(("groups", "tm"), "chan", "space", None),
            P("chan", None),
            P("space", None),
            P(None, ("space", "chan")),
            P(),
            P(),
            P(),
            P(),
            P("groups"),
            P("groups", None),
            P(("groups", "tm")),
        ),
        out_specs=(
            P(("groups", "tm"), None),
            P(("groups", "tm"), None, None),
            P(("groups", "tm"), "chan", None),
        ),
        check_vma=False,
    )
```
